128 devices in a mesh: chain: 16 (over y_hi, x, core), lane: 8 (over z, y_lo).
Axes of the slice: x: 4, y: 4 (y_hi: 2, y_lo: 2; y = y_hi * 2 + y_lo), z: 4, core: 2. Of those that a mesh axis runs over, the one named last changes fastest.
Arguments:
- fiedler: float32 [16, 192, 256, 128], P(None, 'chain', 'lane'), may hold values from -6 to 6
- side_labels: int32 [192, 256, 128], P('chain', 'lane'), may hold values from 0 to 1, as said below
Outputs:
- squared_image: float32 [16, 240, 256, 128], P(None, 'chain', 'lane')
- gram_blocks: float32 [2, 16, 16], replicated
The draws below stay inside these ranges and needn't reach their ends.
Inputs may be any that keep to these rules, and one draw needn't show every extreme that they name: `side_labels`: along every line of the first dimension (fixed second and third index) the vertices of side 0 form one run of planes [a, b) with 36 <= a <= 60 and 132 <= b <= 156; all other vertices are of side 1.
All inputs are finite; a program needn't handle non-finite values.
Results may differ from the reference program's by a relative error of at most 0.0001.
Values sent between devices are 32-bit elements; how exact they have to be, the bound alone decides.
No kernel may reach another device: no remote copies, remote signals or barrier semaphores. Data moves between devices by JAX's collectives and lax.ppermute only.
A program may use at most 128 MiB of HBM per device.

```python
import jax
import jax.numpy as jnp
from jax import lax

K = 16
NZ = 128
MARGIN = 12
NX = 192
NY = 256
BAND = 120


def draw_side_labels(key, part):
    key_low = jax.random.fold_in(key, 11)
    key_high = jax.random.fold_in(key, 23)
    shift_low = jax.random.randint(key_low, (NY, NZ), -MARGIN, MARGIN + 1)
    shift_high = jax.random.randint(key_high, (NY, NZ), -MARGIN, MARGIN + 1)
    planes = jnp.arange(NX, dtype=jnp.int32)[:, None, None]
    lower_edge = NX // 4 + shift_low
    upper_edge = 3 * NX // 4 + shift_high
    inside = (planes >= lower_edge[None]) & (planes < upper_edge[None])
    return jnp.where(inside, 0, 1).astype(jnp.int32)


def block_levels(key, extent, split, smallest, largest):
    def one(dim, blocks):
        draws = jax.random.uniform(jax.random.fold_in(jax.random.fold_in(key, 6), dim), (blocks,), jnp.float32, smallest / len(split), largest / len(split))
        return jnp.repeat(jnp.exp(draws), extent[dim] // blocks).reshape((-1,) + (1,) * (len(extent) - dim - 1))

    factor_of = one(*split[0])
    for cut in split[1:]:
        factor_of = factor_of * one(*cut)
    return factor_of


def bell_draw(stream_key, extent, spread, reach, split=(), held_as=jnp.bfloat16):
    array = spread * jax.random.normal(stream_key, extent, jnp.float32)
    if split:
        array = array * block_levels(stream_key, extent, split, -0.22, 0.18)
    return jnp.clip(array, -reach, reach).astype(held_as)


def setup_inputs(seed: int = 0) -> dict:
    key_of = jax.random.split(jax.random.key(seed), 3)
    fiedler = bell_draw(key_of[0], (K, NX, NY, NZ), 1.0, 6.0, ((1, 16), (2, 8)), jnp.float32)
    side_labels = draw_side_labels(jax.random.fold_in(key_of[2], 71), 0)
    return dict(fiedler=fiedler, side_labels=side_labels)


def neighbour_sum(field):
    padded = jnp.pad(field, ((0, 0), (1, 1), (0, 0), (0, 0)))
    total = padded[:, :-2] + padded[:, 2:]
    total = total + jnp.roll(field, 1, 2) + jnp.roll(field, -1, 2)
    total = total + jnp.roll(field, 1, 3) + jnp.roll(field, -1, 3)
    return total


def reference(fiedler, side_labels):
    images = []
    grams = []
    for half_idx in range(2):
        start_plane = NX // 4 - MARGIN + half_idx * (NX // 2)
        rolled = jnp.roll(fiedler, -start_plane, axis=1)[:, :BAND]
        labels_band = jnp.roll(side_labels, -start_plane, axis=0)[:BAND]
        keep = labels_band == half_idx
        member = keep.astype(jnp.float32)[None]
        moved = jnp.where(keep[None], rolled, jnp.float32(0.0))
        degree = neighbour_sum(member)
        once_applied = member * (degree * moved - neighbour_sum(moved)) / 6.0
        twice_applied = member * (degree * once_applied - neighbour_sum(once_applied)) / 6.0
        gram = jnp.einsum("kpyz,lpyz->kl", once_applied, once_applied, precision=lax.Precision.HIGHEST)
        images.append(twice_applied)
        grams.append(gram / (BAND * NY * NZ))
    joined = jnp.concatenate(images, axis=1)
    return jnp.roll(joined, BAND // 2, axis=1), jnp.stack(grams)
```

```python
import functools

import jax
import jax.numpy as jnp
from jax import lax
from jax.experimental import pallas as pl
from jax.experimental.pallas import tpu as pltpu
from jax.sharding import Mesh
from jax.sharding import PartitionSpec as P

CHAIN = ("y_far", "x", "core")
LANE = ("z", "y_near")
K = 16
PLANES = 12
BAND = 15
ROWS = 32
COLS = 128
WINDOW = BAND + 4
PADDED = 2 * PLANES + 4
TALL = ROWS + 8
CUTS = ((0, 12), (12, 16))
SIXTH = 1.0 / 6.0
TOTAL = 3932160.0
VMEM_LIMIT = 50 * 1024 * 1024

ACROSS = [(c, (c - 1) % 16 if c % 2 == 0 else (c + 1) % 16) for c in range(16)]
ON_CHIP = [(c, c ^ 1) for c in range(16)]
NEEDS_ACROSS = (4, 6, 12, 14, 1, 3, 9, 11)
BULK_ACROSS = [(s, t) for s, t in ACROSS if t in NEEDS_ACROSS]


def full_spec():
    return pl.BlockSpec(memory_space=pltpu.VMEM)


def smem_spec():
    return pl.BlockSpec(memory_space=pltpu.SMEM)


def pack_kernel(flags, field, labels, edge, up, down):
    first = flags[0] * (PLANES - 2)

    def one(k, carry):
        for j in range(2):
            edge[2 * k + j] = field[k, first + j]
        for p in range(PLANES):
            up[k, p] = field[k, p, ROWS - 2 :, :]
            down[k, p] = field[k, p, :2, :]
        return carry

    lax.fori_loop(0, K, one, 0)
    for p in range(PLANES):
        marks = labels[p].astype(jnp.float32)
        edge[2 * K + p] = marks
        up[K, p] = marks[ROWS - 2 :, :]
        down[K, p] = marks[:2, :]


def apply_edges(here, ex, ex_before, wy, wz):
    rows = here.shape[0]
    ey = wy * (here - pltpu.roll(here, rows - 1, 0))
    ez = wz * (here - pltpu.roll(here, COLS - 1, 1))
    return (ex - ex_before) + (ey - pltpu.roll(ey, 1, 0)) + (ez - pltpu.roll(ez, 1, 1))


def gram_kernel(
    flags, field, labels, edge, core_field, core_labels, low, high, out,
    marks, wx, wy, wz, tiles, once, rows,
):
    odd = flags[0]
    is_odd = odd == 1
    same = lambda a, b: jnp.where(a == b, jnp.float32(SIXTH), jnp.float32(0.0))
    tiles[...] = jnp.zeros_like(tiles)
    for p in range(PLANES):
        marks[p, :ROWS] = labels[p].astype(jnp.float32)
        marks[p, ROWS:] = jnp.full((8, COLS), -1.0, jnp.float32)
        marks[p, ROWS : ROWS + 2] = high[K, p]
        marks[p, TALL - 2 :] = low[K, p]
    across_marks = edge[2 * K + (PLANES - 1) * (1 - odd)]
    core_marks = core_labels[(PLANES - 1) * odd].astype(jnp.float32)
    marks_low = jnp.where(is_odd, core_marks, across_marks)
    marks_high = jnp.where(is_odd, across_marks, core_marks)
    wx[0] = same(marks_low, marks[0, :ROWS])
    for p in range(PLANES):
        here = marks[p]
        after = marks[p + 1, :ROWS] if p + 1 < PLANES else marks_high
        wx[p + 1] = same(here[:ROWS], after)
        wy[p] = same(here, pltpu.roll(here, TALL - 1, 0))
        wz[p] = same(here[:ROWS], pltpu.roll(here[:ROWS], COLS - 1, 1))

    def one(k, carry):
        across = edge[2 * k + 1 - odd]
        core = core_field[k, 0]
        before = jnp.where(is_odd, core, across)
        last = jnp.where(is_odd, across, core)
        for p in range(PLANES):
            tiles[p, :2] = high[k, p]
            tiles[p, 6:] = low[k, p]
        here = field[k, 0]
        ex_before = wx[0] * (before - here)
        for p in range(PLANES):
            after = field[k, p + 1] if p + 1 < PLANES else last
            ex = wx[p + 1] * (here - after)
            tall = jnp.concatenate([here, tiles[p]], axis=0)
            ey = wy[p] * (tall - pltpu.roll(tall, TALL - 1, 0))
            ey = (ey - pltpu.roll(ey, 1, 0))[:ROWS]
            ez = wz[p] * (here - pltpu.roll(here, COLS - 1, 1))
            once[k, p] = (ex - ex_before) + ey + (ez - pltpu.roll(ez, 1, 1))
            here, ex_before = after, ex
        return carry

    lax.fori_loop(0, K, one, 0)

    rows[...] = jnp.zeros_like(rows)
    groups = []
    for base in (0, 8):
        groups.append([(base + i, base + j) for i in range(8) for j in range(i, 8)])
    for base in (8, 12):
        groups.append([(i, base + j) for i in range(8) for j in range(4)])
    for side in range(2):

        @pl.when(flags[1 + side] == 1)
        def _():
            for pairs in groups:
                lefts = sorted({a for a, _ in pairs})
                both = sorted({a for a, _ in pairs} | {b for _, b in pairs})

                def plane(p, sums):
                    sums = list(sums)
                    for t in range(ROWS // 8):
                        window = slice(8 * t, 8 * t + 8)
                        keep = marks[p, window] == jnp.float32(side)
                        values = {k: once[k, p, window] for k in both}
                        kept = {
                            k: jnp.where(keep, values[k], jnp.float32(0.0)) for k in lefts
                        }
                        for n, (a, b) in enumerate(pairs):
                            sums[n] = sums[n] + kept[a] * values[b]
                    return tuple(sums)

                zero = jnp.zeros((8, COLS), jnp.float32)
                sums = lax.fori_loop(0, PLANES, plane, (zero,) * len(pairs))
                for n, (a, b) in enumerate(pairs):
                    line = jnp.sum(sums[n], axis=0, keepdims=True)
                    rows[pl.ds(side * 256 + a * 16 + b, 1)] = line
                    if a != b:
                        rows[pl.ds(side * 256 + b * 16 + a, 1)] = line

    ones = jnp.full((8, COLS), 1.0, jnp.float32)
    total = lax.dot_general(
        ones, rows[...], (((1,), (1,)), ((), ())),
        precision=lax.Precision.HIGHEST, preferred_element_type=jnp.float32,
    )
    out[...] = total[:1] * jnp.float32(1.0 / TOTAL)


def band_kernel(
    base, count, flags, field, across, core, labels, edge, core_labels,
    low, high, across_lines, core_lines, *rest,
):
    out, marks, wx, wy, wz, window, once = rest[-7:]
    odd, is_across, below, offset, side = (flags[i] for i in (0, 3, 4, 5, 6))
    step = pl.program_id(0)
    at_partner = jnp.where(below == 1, 2, 2 + PLANES)
    at_own = jnp.where(below == 1, 2 + PLANES, 2)
    at_extra = jnp.where(below == 1, 2 + 2 * PLANES, 0)
    extra_first = (1 - odd) * (PLANES - 2)

    def put_lines(where, index, lines, k, p):
        where[index, ROWS : ROWS + 2] = lines[K + 1 + k, p]
        where[index, TALL - 2 :] = lines[k, p]

    def fill(where, k, own, partner_a, partner_c, extra):
        for p in range(PLANES):
            where[at_own + p, :ROWS] = own(p)
            where[at_own + p, ROWS : ROWS + 2] = high[k, p]
            where[at_own + p, TALL - 2 :] = low[k, p]
        for j in range(2):
            where[at_extra + j, :ROWS] = extra(j)
            put_lines(where, at_extra + j, across_lines, k, extra_first + j)

        @pl.when(is_across == 1)
        def _():
            for p in range(PLANES):
                where[at_partner + p, :ROWS] = partner_a(p)
                put_lines(where, at_partner + p, across_lines, k, p)

        @pl.when(is_across == 0)
        def _():
            for p in range(PLANES):
                where[at_partner + p, :ROWS] = partner_c(p)
                put_lines(where, at_partner + p, core_lines, k, p)

    @pl.when(step == 0)
    def _():
        marks[...] = jnp.full_like(marks, -1.0)
        window[...] = jnp.zeros_like(window)
        fill(
            marks, K,
            lambda p: labels[p].astype(jnp.float32),
            lambda p: edge[2 * K + p],
            lambda p: core_labels[p].astype(jnp.float32),
            lambda j: edge[2 * K + extra_first + j],
        )
        wanted = side.astype(jnp.float32)

        def member(j):
            return jnp.where(marks[offset + j] == wanted, jnp.float32(1.0), jnp.float32(0.0))

        here = member(0)
        for j in range(WINDOW - 1):
            after = member(j + 1)
            scaled = here * jnp.float32(SIXTH)
            wx[j] = scaled * after
            wy[j] = scaled * pltpu.roll(here, TALL - 1, 0)
            wz[j] = scaled * pltpu.roll(here, COLS - 1, 1)
            here = after

    def one(i, carry):
        k = base + step * count + i
        fill(
            window, k,
            lambda p: field[i, p],
            lambda p: across[i, p],
            lambda p: core[i, p],
            lambda j: edge[2 * k + j],
        )
        here = window[offset + 1]
        ex_before = wx[0] * (window[offset] - here)
        for j in range(1, WINDOW - 1):
            after = window[offset + j + 1]
            ex = wx[j] * (here - after)
            once[j] = apply_edges(here, ex, ex_before, wy[j], wz[j])
            here, ex_before = after, ex
        here = once[2]
        ex_before = wx[1] * (once[1] - here)
        for j in range(2, WINDOW - 2):
            after = once[j + 1]
            ex = wx[j] * (here - after)
            out[i, j - 2] = apply_edges(here, ex, ex_before, wy[j], wz[j])[:ROWS]
            here, ex_before = after, ex
        return carry

    lax.fori_loop(0, count, one, 0)


def band(flags, field, across, core, labels, edge, core_labels, low, high,
         across_lines, core_lines, lo, hi, previous):
    count = 2
    steps = (hi - lo) // count
    start = lo // count
    block = (count, PLANES, ROWS, COLS)
    here = pl.BlockSpec(block, lambda i: (start + i, 0, 0, 0))
    whole = [full_spec()] * 7
    args = [flags, field, across, core, labels, edge, core_labels, low, high,
            across_lines, core_lines]
    in_specs = [smem_spec(), here, pl.BlockSpec(block, lambda i: (i, 0, 0, 0)), here] + whole
    aliases = {}
    if previous is not None:
        args.append(previous)
        in_specs.append(pl.BlockSpec(memory_space=pl.ANY))
        aliases = {len(args) - 1: 0}
    return pl.pallas_call(
        functools.partial(band_kernel, lo, count),
        grid=(steps,),
        in_specs=in_specs,
        out_specs=pl.BlockSpec((count, BAND, ROWS, COLS), lambda i: (start + i, 0, 0, 0)),
        out_shape=jax.ShapeDtypeStruct((K, BAND, ROWS, COLS), jnp.float32),
        scratch_shapes=[
            pltpu.VMEM((PADDED, TALL, COLS), jnp.float32),
            pltpu.VMEM((WINDOW, TALL, COLS), jnp.float32),
            pltpu.VMEM((WINDOW, TALL, COLS), jnp.float32),
            pltpu.VMEM((WINDOW, TALL, COLS), jnp.float32),
            pltpu.VMEM((PADDED, TALL, COLS), jnp.float32),
            pltpu.VMEM((WINDOW, TALL, COLS), jnp.float32),
        ],
        input_output_aliases=aliases,
        compiler_params=pltpu.CompilerParams(vmem_limit_bytes=VMEM_LIMIT),
        cost_estimate=pl.CostEstimate(
            flops=40 * (hi - lo) * WINDOW * TALL * COLS,
            bytes_accessed=4 * (hi - lo) * (3 * PLANES + BAND) * ROWS * COLS,
            transcendentals=0,
        ),
        name=f"band_{lo}_{hi}",
    )(*args)


def per_device(field, labels):
    c = lax.axis_index(CHAIN)
    odd = c % 2
    below = (c // 4) % 2
    is_across = jnp.where(below == 1, 1 - odd, odd)
    side = jnp.where((c >= 4) & (c < 12), 0, 1)
    has_first = ((c >= 3) & (c <= 12)).astype(jnp.int32)
    has_second = ((c <= 4) | (c >= 11)).astype(jnp.int32)
    flags = jnp.stack(
        [odd, has_first, has_second, is_across, below, 3 * (c % 4), side]
    ).astype(jnp.int32)

    lines = jax.ShapeDtypeStruct((K + 1, PLANES, 2, COLS), jnp.float32)
    edge, up, down = pl.pallas_call(
        pack_kernel,
        in_specs=[smem_spec(), full_spec(), full_spec()],
        out_specs=[full_spec()] * 3,
        out_shape=[
            jax.ShapeDtypeStruct((2 * K + PLANES, ROWS, COLS), jnp.float32), lines, lines,
        ],
        compiler_params=pltpu.CompilerParams(vmem_limit_bytes=VMEM_LIMIT),
        name="pack",
    )(flags, field, labels)

    ring = [(i, (i + 1) % 8) for i in range(8)]
    back = [(t, s) for s, t in ring]
    core = lax.ppermute(field, CHAIN, ON_CHIP)
    core_labels = lax.ppermute(labels, CHAIN, ON_CHIP)
    edge = lax.ppermute(edge, CHAIN, ACROSS)
    low = lax.ppermute(up, LANE, ring)
    high = lax.ppermute(down, LANE, back)
    across = [lax.ppermute(field[lo:hi], CHAIN, BULK_ACROSS) for lo, hi in CUTS]

    gram = pl.pallas_call(
        gram_kernel,
        grid=(1,),
        in_specs=[
            smem_spec(), full_spec(), full_spec(), full_spec(),
            full_spec(),
            full_spec(), full_spec(), full_spec(),
        ],
        out_specs=full_spec(),
        out_shape=jax.ShapeDtypeStruct((1, 512), jnp.float32),
        scratch_shapes=[
            pltpu.VMEM((PLANES, TALL, COLS), jnp.float32),
            pltpu.VMEM((PLANES + 1, ROWS, COLS), jnp.float32),
            pltpu.VMEM((PLANES, TALL, COLS), jnp.float32),
            pltpu.VMEM((PLANES, ROWS, COLS), jnp.float32),
            pltpu.VMEM((PLANES, 8, COLS), jnp.float32),
            pltpu.VMEM((K, PLANES, ROWS, COLS), jnp.float32),
            pltpu.VMEM((512, COLS), jnp.float32),
        ],
        compiler_params=pltpu.CompilerParams(vmem_limit_bytes=VMEM_LIMIT),
        cost_estimate=pl.CostEstimate(
            flops=60 * K * PLANES * ROWS * COLS, bytes_accessed=8 << 20, transcendentals=0
        ),
        name="gram",
    )(
        flags, field, labels, edge,
        lax.dynamic_slice_in_dim(core, odd * (PLANES - 1), 1, 1),
        core_labels, low, high,
    )

    both_lines = jnp.concatenate([low, high], axis=0)
    across_lines = lax.ppermute(both_lines, CHAIN, ACROSS)
    core_lines = lax.ppermute(both_lines, CHAIN, ON_CHIP)

    def swap(value, axes, size, flip):
        return value + lax.ppermute(value, axes, [(i, i ^ flip) for i in range(size)])

    gram = swap(gram, ("core",), 2, 1)
    gram = swap(gram, ("y_near",), 2, 1)
    gram = swap(gram, ("y_far", "y_near"), 4, 3)
    gram = swap(gram, ("z",), 4, 1)
    gram = swap(gram, ("z",), 4, 3)
    gram = swap(gram, ("x",), 4, 1)
    gram = swap(gram, ("x",), 4, 3)

    image = None
    for (lo, hi), part in zip(CUTS, across):
        image = band(flags, field, part, core, labels, edge, core_labels, low, high,
                     across_lines, core_lines, lo, hi, image)
    return image, gram.reshape(2, K, K)


def solution(mesh):
    finer = Mesh(
        mesh.devices.reshape(2, 4, 2, 4, 2), ("y_far", "x", "core", "z", "y_near")
    )
    return jax.shard_map(
        per_device,
        mesh=finer,
        in_specs=(P(None, CHAIN, LANE, None), P(CHAIN, LANE, None)),
        out_specs=(P(None, CHAIN, LANE, None), P()),
        check_vma=False,
    )
```

```python
import functools

import jax
import jax.numpy as jnp
from jax import lax
from jax.experimental import pallas as pl
from jax.experimental.pallas import tpu as pltpu
from jax.sharding import Mesh
from jax.sharding import PartitionSpec as P

CHAIN = ("y_far", "x", "core")
LANE = ("z", "y_near")
K = 16
PLANES = 12
BAND = 15
STRIP = 2 * PLANES
ROWS = 32
COLS = 128
WINDOW = BAND + 4
PADDED = 2 * PLANES + 4
TALL = ROWS + 8
FOLD = 4
EARLY = 8
PAIR = 2
EDGE = K + PLANES
LINES = (K + 1) * STRIP
FIELD_ROWS = K * PLANES * ROWS
CHEAP = pl.CostEstimate(flops=1000, bytes_accessed=1000, transcendentals=0)
SIXTH = 1.0 / 6.0
TOTAL = 3932160.0
VMEM_LIMIT = 60 * 1024 * 1024

ACROSS = [(c, (c - 1) % 16 if c % 2 == 0 else (c + 1) % 16) for c in range(16)]
ON_CHIP = [(c, c ^ 1) for c in range(16)]
NEEDS_ACROSS = (4, 6, 12, 14, 1, 3, 9, 11)
BULK_ACROSS = [(s, t) for s, t in ACROSS if t in NEEDS_ACROSS]


def roles():
    c = lax.axis_index("y_far") * 8 + lax.axis_index("x") * 2 + lax.axis_index("core")
    odd = lax.rem(c, 2)
    below = lax.rem(c // 4, 2)
    return dict(
        odd=odd,
        below=below,
        is_across=jnp.where(below == 1, 1 - odd, odd),
        offset=3 * lax.rem(c, 4),
        side=jnp.where((c >= 4) & (c < 12), 0, 1),
        has=((c >= 3) & (c <= 12), (c <= 4) | (c >= 11)),
    )


def full_spec():
    return pl.BlockSpec(memory_space=pltpu.VMEM)


def smem_spec():
    return pl.BlockSpec(memory_space=pltpu.SMEM)


def pack_kernel(field, labels, edge, core_edge, up, down, marks, sems):
    odd = roles()["odd"]
    last = PLANES - 1
    copies = [
        pltpu.make_async_copy(field.at[:, odd * last], edge.at[pl.ds(0, K)], sems.at[0]),
        pltpu.make_async_copy(
            field.at[:, (1 - odd) * last], core_edge.at[pl.ds(0, K)], sems.at[1]
        ),
    ]
    for copy in copies:
        copy.start()
    late = [
        pltpu.make_async_copy(marks, edge.at[pl.ds(K, PLANES)], sems.at[2]),
        pltpu.make_async_copy(marks, core_edge.at[pl.ds(K, PLANES)], sems.at[3]),
    ]
    values = [labels[p].astype(jnp.float32) for p in range(PLANES)]
    for p in range(PLANES):
        marks[p] = values[p]
    for copy in late:
        copy.start()
    up[K * STRIP :] = jnp.concatenate([v[ROWS - 2 :] for v in values], axis=0)
    down[K * STRIP :] = jnp.concatenate([v[:2] for v in values], axis=0)

    def one(k, carry):
        strip = pl.ds(pl.multiple_of(k * STRIP, 8), STRIP)
        up[strip] = jnp.concatenate(
            [field[k, p, ROWS - 2 :] for p in range(PLANES)], axis=0
        )
        down[strip] = jnp.concatenate([field[k, p, :2] for p in range(PLANES)], axis=0)
        return carry

    lax.fori_loop(0, K, one, 0)
    for copy in copies + late:
        copy.wait()


def line_sum(here):
    rows = here.shape[0]
    around = pltpu.roll(here, 1, 0) + pltpu.roll(here, rows - 1, 0)
    return around + (pltpu.roll(here, 1, 1) + pltpu.roll(here, COLS - 1, 1))


def gram_kernel(
    field, labels, edge, core_edge, low, high, out, lines_out,
    marks, weights, tiles, once, rows, sems,
):
    role = roles()
    odd = role["odd"]
    is_odd = odd == 1
    step = pl.program_id(0)
    steps = K // FOLD
    same = lambda a, b: jnp.where(a == b, jnp.float32(SIXTH), jnp.float32(0.0))
    joins = [
        pltpu.make_async_copy(low, lines_out.at[pl.ds(0, LINES)], sems.at[0]),
        pltpu.make_async_copy(high, lines_out.at[pl.ds(LINES, LINES)], sems.at[1]),
    ]

    following = 1 + odd * (PLANES - 3)
    extras = [
        pltpu.make_async_copy(
            field.at[pl.ds(pl.multiple_of((i * PLANES + following) * ROWS, 8), ROWS)],
            lines_out.at[
                pl.ds(pl.multiple_of(2 * LINES + (step * FOLD + i) * ROWS, 8), ROWS)
            ],
            sems.at[2 + i],
        )
        for i in range(FOLD)
    ]
    for extra in extras:
        extra.start()

    @pl.when(step == 0)
    def _():
        for join in joins:
            join.start()
        tiles[...] = jnp.zeros_like(tiles)
        for p in range(PLANES):
            first = K * STRIP + 2 * p
            marks[p, :ROWS] = labels[p].astype(jnp.float32)
            marks[p, ROWS:] = jnp.full((8, COLS), -1.0, jnp.float32)
            marks[p, ROWS : ROWS + 2] = high[first : first + 2]
            marks[p, TALL - 2 :] = low[first : first + 2]
        across_marks = edge[K + (PLANES - 1) * (1 - odd)]
        core_marks = core_edge[K + (PLANES - 1) * odd]
        marks_low = jnp.where(is_odd, core_marks, across_marks)
        marks_high = jnp.where(is_odd, across_marks, core_marks)
        for p in range(PLANES):
            tall = marks[p]
            here = tall[:ROWS]
            around = (
                marks[p - 1, :ROWS] if p else marks_low,
                marks[p + 1, :ROWS] if p + 1 < PLANES else marks_high,
                pltpu.roll(tall, 1, 0)[:ROWS],
                pltpu.roll(tall, TALL - 1, 0)[:ROWS],
                pltpu.roll(here, 1, 1),
                pltpu.roll(here, COLS - 1, 1),
            )
            degree = jnp.zeros((ROWS, COLS), jnp.float32)
            for n, other in enumerate(around):
                weight = same(here, other)
                weights[n, p] = weight
                degree = degree + weight
            weights[6, p] = degree

    def one(i, carry):
        k = step * FOLD + i
        across = edge[k]
        core = core_edge[k]
        before = jnp.where(is_odd, core, across)
        last = jnp.where(is_odd, across, core)
        strip = pl.ds(pl.multiple_of(k * STRIP, 8), STRIP)
        after_lines, before_lines = high[strip], low[strip]
        for p in range(PLANES):
            tiles[p, :2] = after_lines[2 * p : 2 * p + 2]
            tiles[p, 6:] = before_lines[2 * p : 2 * p + 2]
        plane = lambda p: field[pl.ds(pl.multiple_of((i * PLANES + p) * ROWS, 8), ROWS)]
        here = plane(0)
        for p in range(PLANES):
            after = plane(p + 1) if p + 1 < PLANES else last
            tall = jnp.concatenate([here, tiles[p]], axis=0)
            value = weights[6, p] * here
            value = value - (weights[0, p] * before + weights[1, p] * after)
            value = value - (
                weights[2, p] * pltpu.roll(tall, 1, 0)[:ROWS]
                + weights[3, p] * pltpu.roll(tall, TALL - 1, 0)[:ROWS]
            )
            once[k, p] = value - (
                weights[4, p] * pltpu.roll(here, 1, 1)
                + weights[5, p] * pltpu.roll(here, COLS - 1, 1)
            )
            before, here = here, after
        return carry

    lax.fori_loop(0, FOLD, one, 0)
    for extra in extras:
        extra.wait()

    @pl.when(step == steps - 1)
    def _():
        sum_pairs(role, out, marks, once, rows)
        for join in joins:
            join.wait()


def sum_pairs(role, out, marks, once, rows):
    rows[...] = jnp.zeros_like(rows)
    groups = []
    for base in (0, 8):
        groups.append([(base + i, base + j) for i in range(8) for j in range(i, 8)])
    for base in (8, 12):
        groups.append([(i, base + j) for i in range(8) for j in range(4)])
    for side in range(2):

        @pl.when(role["has"][side])
        def _():
            for pairs in groups:
                lefts = sorted({a for a, _ in pairs})
                both = sorted({a for a, _ in pairs} | {b for _, b in pairs})

                def plane(p, sums):
                    sums = list(sums)
                    for t in range(ROWS // 8):
                        window = slice(8 * t, 8 * t + 8)
                        keep = marks[p, window] == jnp.float32(side)
                        values = {k: once[k, p, window] for k in both}
                        kept = {
                            k: jnp.where(keep, values[k], jnp.float32(0.0)) for k in lefts
                        }
                        for n, (a, b) in enumerate(pairs):
                            sums[n] = sums[n] + kept[a] * values[b]
                    return tuple(sums)

                zero = jnp.zeros((8, COLS), jnp.float32)
                sums = lax.fori_loop(0, PLANES, plane, (zero,) * len(pairs))
                for n, (a, b) in enumerate(pairs):
                    line = jnp.sum(sums[n], axis=0, keepdims=True)
                    rows[pl.ds(side * 256 + a * 16 + b, 1)] = line
                    if a != b:
                        rows[pl.ds(side * 256 + b * 16 + a, 1)] = line

    total = jnp.sum(rows[...].T, axis=0, keepdims=True)
    out[...] = total * jnp.float32(1.0 / TOTAL)


def band_kernel(
    field, across_first, across_last, core, labels, edge, core_edge,
    low, high, lines_across, lines_core, out,
    marks, centre, around, window, once,
):
    role = roles()
    odd, is_across, below = role["odd"], role["is_across"], role["below"]
    offset, side = role["offset"], role["side"]
    step = pl.program_id(0)
    at_partner = jnp.where(below == 1, 2, 2 + PLANES)
    at_own = jnp.where(below == 1, 2 + PLANES, 2)
    at_extra = jnp.where(below == 1, 2 + 2 * PLANES, 0)
    at_boundary = at_partner + (1 - odd) * (PLANES - 1)
    boundary = (1 - odd) * (PLANES - 1)
    following = 1 + (1 - odd) * (PLANES - 3)

    def put_lines(where, index, before, after, p):
        where[index, ROWS : ROWS + 2] = after[2 * p : 2 * p + 2]
        where[index, TALL - 2 :] = before[2 * p : 2 * p + 2]

    def strips(lines, k):
        first = pl.multiple_of(k * STRIP, 8)
        return lines[pl.ds(first, STRIP)], lines[pl.ds(first + LINES, STRIP)]

    def fill_lines(where, k):
        own = pl.ds(pl.multiple_of(k * STRIP, 8), STRIP)
        before, after = low[own], high[own]
        for p in range(PLANES):
            put_lines(where, at_own + p, before, after, p)
        for index, p in ((at_extra + 1 - odd, boundary), (at_extra + odd, following)):
            first = k * STRIP + 2 * p
            where[index, TALL - 2 :] = lines_across[pl.ds(first, 2)]
            where[index, ROWS : ROWS + 2] = lines_across[pl.ds(first + LINES, 2)]

        @pl.when(is_across == 1)
        def _():
            before, after = strips(lines_across, k)
            for p in range(PLANES):
                put_lines(where, at_partner + p, before, after, p)

        @pl.when(is_across == 0)
        def _():
            before, after = strips(lines_core, k)
            for p in range(PLANES):
                put_lines(where, at_partner + p, before, after, p)

    @pl.when(step == 0)
    def _():
        marks[...] = jnp.full_like(marks, -1.0)
        window[...] = jnp.zeros_like(window)
        fill_lines(marks, K)
        for p in range(PLANES):
            marks[at_own + p, :ROWS] = labels[p].astype(jnp.float32)
            marks[at_partner + p, :ROWS] = jnp.where(
                is_across == 1, edge[K + p], core_edge[K + p]
            )
        marks[at_extra + 1 - odd, :ROWS] = edge[K + boundary]
        marks[at_extra + odd, :ROWS] = edge[K + following]
        wanted = side.astype(jnp.float32)
        for j in range(PADDED):
            marks[j] = jnp.where(marks[j] == wanted, jnp.float32(1.0), jnp.float32(0.0))
        for j in range(1, WINDOW - 1):
            here = marks[offset + j]
            degree = marks[offset + j - 1] + marks[offset + j + 1] + line_sum(here)
            scaled = here * jnp.float32(SIXTH)
            around[j] = scaled
            centre[j] = scaled * degree

    early = step < EARLY // PAIR

    def one(i, carry):
        k = step * PAIR + i
        fill_lines(window, k)
        for p in range(PLANES):
            window[at_own + p, :ROWS] = field[i, p]
        window[at_extra + 1 - odd, :ROWS] = edge[k]
        window[at_extra + odd, :ROWS] = lines_across[
            pl.ds(pl.multiple_of(2 * LINES + k * ROWS, 8), ROWS)
        ]

        def from_across(source):
            @pl.when(is_across == 1)
            def _():
                for p in range(PLANES - 1):
                    window[at_partner + odd + p, :ROWS] = source[i, p]

        @pl.when(early)
        def _():
            from_across(across_first)

        @pl.when(jnp.logical_not(early))
        def _():
            from_across(across_last)

        @pl.when(is_across == 1)
        def _():
            window[at_boundary, :ROWS] = edge[k]

        @pl.when(is_across == 0)
        def _():
            for p in range(PLANES):
                window[at_partner + p, :ROWS] = core[i, p]

        before = window[offset] * marks[offset]
        here = window[offset + 1] * marks[offset + 1]
        for j in range(1, WINDOW - 1):
            after = window[offset + j + 1] * marks[offset + j + 1]
            once[j] = centre[j] * here - around[j] * (before + after + line_sum(here))
            before, here = here, after
        for j in range(2, WINDOW - 2):
            here = once[j]
            total = once[j - 1] + once[j + 1] + line_sum(here)
            out[i, j - 2] = (centre[j] * here - around[j] * total)[:ROWS]
        return carry

    lax.fori_loop(0, PAIR, one, 0)


def band(field, across_first, across_last, core, labels, edge, core_edge, low, high,
         lines_across, lines_core):
    return pl.pallas_call(
        band_kernel,
        grid=(K // PAIR,),
        in_specs=[
            pl.BlockSpec((PAIR, PLANES, ROWS, COLS), lambda i: (i, 0, 0, 0)),
            pl.BlockSpec(
                (PAIR, PLANES - 1, ROWS, COLS),
                lambda i: (jnp.minimum(i, EARLY // PAIR - 1), 0, 0, 0),
            ),
            pl.BlockSpec(
                (PAIR, PLANES - 1, ROWS, COLS),
                lambda i: (jnp.maximum(i - EARLY // PAIR, 0), 0, 0, 0),
            ),
            pl.BlockSpec((PAIR, PLANES, ROWS, COLS), lambda i: (i, 0, 0, 0)),
            full_spec(), full_spec(), full_spec(), full_spec(), full_spec(),
            full_spec(), full_spec(),
        ],
        out_specs=pl.BlockSpec((PAIR, BAND, ROWS, COLS), lambda i: (i, 0, 0, 0)),
        out_shape=jax.ShapeDtypeStruct((K, BAND, ROWS, COLS), jnp.float32),
        scratch_shapes=[
            pltpu.VMEM((PADDED, TALL, COLS), jnp.float32),
            pltpu.VMEM((WINDOW, TALL, COLS), jnp.float32),
            pltpu.VMEM((WINDOW, TALL, COLS), jnp.float32),
            pltpu.VMEM((PADDED, TALL, COLS), jnp.float32),
            pltpu.VMEM((WINDOW, TALL, COLS), jnp.float32),
        ],
        compiler_params=pltpu.CompilerParams(vmem_limit_bytes=VMEM_LIMIT),
        cost_estimate=CHEAP,
        name="band",
    )(field, across_first, across_last, core, labels, edge, core_edge, low, high,
      lines_across, lines_core)


def pack(field, labels):
    lines = jax.ShapeDtypeStruct((LINES, COLS), jnp.float32)
    hbm = pl.BlockSpec(memory_space=pl.ANY)
    return pl.pallas_call(
        pack_kernel,
        in_specs=[full_spec(), full_spec()],
        out_specs=[hbm, hbm, full_spec(), full_spec()],
        out_shape=[
            jax.ShapeDtypeStruct((EDGE, ROWS, COLS), jnp.float32),
            jax.ShapeDtypeStruct((EDGE, ROWS, COLS), jnp.float32),
            lines, lines,
        ],
        scratch_shapes=[
            pltpu.VMEM((PLANES, ROWS, COLS), jnp.float32),
            pltpu.SemaphoreType.DMA((4,)),
        ],
        compiler_params=pltpu.CompilerParams(vmem_limit_bytes=VMEM_LIMIT),
        cost_estimate=CHEAP,
        name="pack",
    )(field, labels)


def trim_kernel(field, first, last, sems):
    odd = roles()["odd"]
    planes = pl.ds(1 - odd, PLANES - 1)
    copies = [
        pltpu.make_async_copy(field.at[pl.ds(0, EARLY), planes], first, sems.at[0]),
        pltpu.make_async_copy(field.at[pl.ds(EARLY, K - EARLY), planes], last, sems.at[1]),
    ]
    for copy in copies:
        copy.start()
    for copy in copies:
        copy.wait()


def trim(field):
    hbm = pl.BlockSpec(memory_space=pl.ANY)
    return pl.pallas_call(
        trim_kernel,
        in_specs=[full_spec()],
        out_specs=[hbm, hbm],
        out_shape=[
            jax.ShapeDtypeStruct((EARLY, PLANES - 1, ROWS, COLS), jnp.float32),
            jax.ShapeDtypeStruct((K - EARLY, PLANES - 1, ROWS, COLS), jnp.float32),
        ],
        scratch_shapes=[pltpu.SemaphoreType.DMA((2,))],
        compiler_params=pltpu.CompilerParams(vmem_limit_bytes=VMEM_LIMIT),
        cost_estimate=CHEAP,
        name="trim",
    )(field)


def gram_terms(field, labels, edge, core_edge, low, high):
    hbm = pl.BlockSpec(memory_space=pl.ANY)
    return pl.pallas_call(
        gram_kernel,
        grid=(K // FOLD,),
        in_specs=[
            pl.BlockSpec((FOLD * PLANES * ROWS, COLS), lambda i: (i, 0)),
            full_spec(),
        ] + [full_spec()] * 4,
        out_specs=[full_spec(), hbm],
        out_shape=[
            jax.ShapeDtypeStruct((1, 512), jnp.float32),
            jax.ShapeDtypeStruct((2 * LINES + K * ROWS, COLS), jnp.float32),
        ],
        scratch_shapes=[
            pltpu.VMEM((PLANES, TALL, COLS), jnp.float32),
            pltpu.VMEM((7, PLANES, ROWS, COLS), jnp.float32),
            pltpu.VMEM((PLANES, 8, COLS), jnp.float32),
            pltpu.VMEM((K, PLANES, ROWS, COLS), jnp.float32),
            pltpu.VMEM((512, COLS), jnp.float32),
            pltpu.SemaphoreType.DMA((2 + FOLD,)),
        ],
        compiler_params=pltpu.CompilerParams(vmem_limit_bytes=VMEM_LIMIT),
        cost_estimate=CHEAP,
        name="gram",
    )(field.reshape(FIELD_ROWS, COLS), labels, edge, core_edge, low, high)


def per_device(field, labels):
    edge, core_edge, up, down = pack(field, labels)
    ring = [(i, (i + 1) % 8) for i in range(8)]
    back = [(t, s) for s, t in ring]
    low = lax.ppermute(up, LANE, ring)
    high = lax.ppermute(down, LANE, back)
    edge = lax.ppermute(edge, CHAIN, ACROSS)
    core_edge = lax.ppermute(core_edge, CHAIN, ON_CHIP)
    later, _ = lax.optimization_barrier((field, core_edge))
    first, last = trim(later)
    across_first = lax.ppermute(first, CHAIN, BULK_ACROSS)
    core = lax.ppermute(field, CHAIN, ON_CHIP)

    gram, both_lines = gram_terms(field, labels, edge, core_edge, low, high)
    last, _ = lax.optimization_barrier((last, gram))
    lines_across = lax.ppermute(both_lines, CHAIN, ACROSS)
    across_last = lax.ppermute(last, CHAIN, BULK_ACROSS)
    lines_core = lax.ppermute(both_lines, CHAIN, ON_CHIP)

    def swap(value, axes, size, flip):
        return value + lax.ppermute(value, axes, [(i, i ^ flip) for i in range(size)])

    gram, across_first = lax.optimization_barrier((gram, across_first))
    gram = swap(gram, ("core",), 2, 1)
    gram = swap(gram, ("y_near",), 2, 1)
    gram = swap(gram, ("y_far", "y_near"), 4, 3)
    gram = swap(gram, ("z",), 4, 1)
    gram = swap(gram, ("z",), 4, 3)
    gram = swap(gram, ("x",), 4, 1)
    gram = swap(gram, ("x",), 4, 3)

    image = band(field, across_first, across_last, core, labels, edge, core_edge, low, high,
                 lines_across, lines_core)
    return image, gram.reshape(2, K, K)


def solution(mesh):
    finer = Mesh(
        mesh.devices.reshape(2, 4, 2, 4, 2), ("y_far", "x", "core", "z", "y_near")
    )
    return jax.shard_map(
        per_device,
        mesh=finer,
        in_specs=(P(None, CHAIN, LANE, None), P(CHAIN, LANE, None)),
        out_specs=(P(None, CHAIN, LANE, None), P()),
        check_vma=False,
    )
```

```python
import functools

import jax
import jax.numpy as jnp
from jax import lax
from jax.experimental import pallas as pl
from jax.experimental.pallas import tpu as pltpu
from jax.sharding import Mesh
from jax.sharding import PartitionSpec as P

CHAIN = ("y_far", "x", "core")
LANE = ("z", "y_near")
K = 16
PLANES = 12
BAND = 15
STRIP = 2 * PLANES
ROWS = 32
COLS = 128
WINDOW = BAND + 4
PADDED = 2 * PLANES + 4
TALL = ROWS + 8
FOLD = 4
EARLY = 8
PAIR = 4
EDGE = K + 1
LINES = (K + 1) * STRIP
AT_EXTRA = 2 * LINES
AT_MARKS = AT_EXTRA + K * ROWS
MESSAGE = AT_MARKS + PLANES * ROWS
FIELD_ROWS = K * PLANES * ROWS
CHEAP = pl.CostEstimate(flops=1000, bytes_accessed=1000, transcendentals=0)
SIXTH = 1.0 / 6.0
TOTAL = 3932160.0
VMEM_LIMIT = 60 * 1024 * 1024

ACROSS = [(c, (c - 1) % 16 if c % 2 == 0 else (c + 1) % 16) for c in range(16)]
ON_CHIP = [(c, c ^ 1) for c in range(16)]
NEEDS_ACROSS = (4, 6, 12, 14, 1, 3, 9, 11)
BULK_ACROSS = [(s, t) for s, t in ACROSS if t in NEEDS_ACROSS]


def roles():
    c = lax.axis_index("y_far") * 8 + lax.axis_index("x") * 2 + lax.axis_index("core")
    odd = lax.rem(c, 2)
    below = lax.rem(c // 4, 2)
    return dict(
        odd=odd,
        below=below,
        is_across=jnp.where(below == 1, 1 - odd, odd),
        offset=3 * lax.rem(c, 4),
        far=(lax.rem(c, 8) == 0) | (lax.rem(c, 8) == 7),
        side=jnp.where((c >= 4) & (c < 12), 0, 1),
        has=((c >= 3) & (c <= 12), (c <= 4) | (c >= 11)),
    )


def full_spec():
    return pl.BlockSpec(memory_space=pltpu.VMEM)


def smem_spec():
    return pl.BlockSpec(memory_space=pltpu.SMEM)


def pack_kernel(field, labels, edge, core_edge, up, down, marks, sems):
    odd = roles()["odd"]
    last = PLANES - 1
    copies = [
        pltpu.make_async_copy(field.at[:, odd * last], edge.at[pl.ds(0, K)], sems.at[0]),
        pltpu.make_async_copy(
            field.at[:, (1 - odd) * last], core_edge.at[pl.ds(0, K)], sems.at[1]
        ),
    ]
    for copy in copies:
        copy.start()
    late = [
        pltpu.make_async_copy(marks.at[odd * last], edge.at[K], sems.at[2]),
        pltpu.make_async_copy(marks.at[(1 - odd) * last], core_edge.at[K], sems.at[3]),
    ]
    values = [labels[p].astype(jnp.float32) for p in range(PLANES)]
    for p in range(PLANES):
        marks[p] = values[p]
    for copy in late:
        copy.start()
    up[K * STRIP :] = jnp.concatenate([v[ROWS - 2 :] for v in values], axis=0)
    down[K * STRIP :] = jnp.concatenate([v[:2] for v in values], axis=0)

    def one(k, carry):
        strip = pl.ds(pl.multiple_of(k * STRIP, 8), STRIP)
        up[strip] = jnp.concatenate(
            [field[k, p, ROWS - 2 :] for p in range(PLANES)], axis=0
        )
        down[strip] = jnp.concatenate([field[k, p, :2] for p in range(PLANES)], axis=0)
        return carry

    lax.fori_loop(0, K, one, 0)
    for copy in copies + late:
        copy.wait()


def line_sum(here):
    rows = here.shape[0]
    around = pltpu.roll(here, 1, 0) + pltpu.roll(here, rows - 1, 0)
    return around + (pltpu.roll(here, 1, 1) + pltpu.roll(here, COLS - 1, 1))


def gram_kernel(
    field, labels, edge, core_edge, low, high, message, out, lines_out,
    marks, weights, tiles, once, rows, sems,
):
    role = roles()
    odd = role["odd"]
    is_odd = odd == 1
    step = pl.program_id(0)
    steps = K // FOLD
    same = lambda a, b: jnp.where(a == b, jnp.float32(SIXTH), jnp.float32(0.0))
    joins = [
        pltpu.make_async_copy(low, lines_out.at[pl.ds(0, LINES)], sems.at[0]),
        pltpu.make_async_copy(high, lines_out.at[pl.ds(LINES, LINES)], sems.at[1]),
    ]

    @pl.when(step == 0)
    def _():
        for join in joins:
            join.start()
        tiles[...] = jnp.zeros_like(tiles)
        for p in range(PLANES):
            first = K * STRIP + 2 * p
            marks[p, :ROWS] = labels[p].astype(jnp.float32)
            marks[p, ROWS:] = jnp.full((8, COLS), -1.0, jnp.float32)
            marks[p, ROWS : ROWS + 2] = high[first : first + 2]
            marks[p, TALL - 2 :] = low[first : first + 2]
        across_marks = edge[K]
        core_marks = core_edge[K]
        marks_low = jnp.where(is_odd, core_marks, across_marks)
        marks_high = jnp.where(is_odd, across_marks, core_marks)
        for p in range(PLANES):
            tall = marks[p]
            here = tall[:ROWS]
            around = (
                marks[p - 1, :ROWS] if p else marks_low,
                marks[p + 1, :ROWS] if p + 1 < PLANES else marks_high,
                pltpu.roll(tall, 1, 0)[:ROWS],
                pltpu.roll(tall, TALL - 1, 0)[:ROWS],
                pltpu.roll(here, 1, 1),
                pltpu.roll(here, COLS - 1, 1),
            )
            degree = jnp.zeros((ROWS, COLS), jnp.float32)
            for n, other in enumerate(around):
                weight = same(here, other)
                weights[n, p] = weight
                degree = degree + weight
            weights[6, p] = degree

    def one(i, carry):
        k = step * FOLD + i
        across = edge[k]
        core = core_edge[k]
        before = jnp.where(is_odd, core, across)
        last = jnp.where(is_odd, across, core)
        strip = pl.ds(pl.multiple_of(k * STRIP, 8), STRIP)
        after_lines, before_lines = high[strip], low[strip]
        for p in range(PLANES):
            tiles[p, :2] = after_lines[2 * p : 2 * p + 2]
            tiles[p, 6:] = before_lines[2 * p : 2 * p + 2]
        plane = lambda p: field[pl.ds(pl.multiple_of((i * PLANES + p) * ROWS, 8), ROWS)]
        here = plane(0)
        for p in range(PLANES):
            after = plane(p + 1) if p + 1 < PLANES else last
            tall = jnp.concatenate([here, tiles[p]], axis=0)
            value = weights[6, p] * here
            value = value - (weights[0, p] * before + weights[1, p] * after)
            value = value - (
                weights[2, p] * pltpu.roll(tall, 1, 0)[:ROWS]
                + weights[3, p] * pltpu.roll(tall, TALL - 1, 0)[:ROWS]
            )
            once[k, p] = value - (
                weights[4, p] * pltpu.roll(here, 1, 1)
                + weights[5, p] * pltpu.roll(here, COLS - 1, 1)
            )
            before, here = here, after
        return carry

    lax.fori_loop(0, FOLD, one, 0)

    @pl.when(step == steps - 1)
    def _():
        sum_pairs(role, out, marks, once, rows)
        for join in joins:
            join.wait()


def sum_pairs(role, out, marks, once, rows):
    rows[...] = jnp.zeros_like(rows)
    groups = []
    for base in (0, 8):
        groups.append([(base + i, base + j) for i in range(8) for j in range(i, 8)])
    for base in (8, 12):
        groups.append([(i, base + j) for i in range(8) for j in range(4)])
    for side in range(2):

        @pl.when(role["has"][side])
        def _():
            for pairs in groups:
                lefts = sorted({a for a, _ in pairs})
                both = sorted({a for a, _ in pairs} | {b for _, b in pairs})

                def plane(p, sums):
                    sums = list(sums)
                    for t in range(ROWS // 8):
                        window = slice(8 * t, 8 * t + 8)
                        keep = marks[p, window] == jnp.float32(side)
                        values = {k: once[k, p, window] for k in both}
                        kept = {
                            k: jnp.where(keep, values[k], jnp.float32(0.0)) for k in lefts
                        }
                        for n, (a, b) in enumerate(pairs):
                            sums[n] = sums[n] + kept[a] * values[b]
                    return tuple(sums)

                zero = jnp.zeros((8, COLS), jnp.float32)
                sums = lax.fori_loop(0, PLANES, plane, (zero,) * len(pairs))
                for n, (a, b) in enumerate(pairs):
                    line = jnp.sum(sums[n], axis=0, keepdims=True)
                    rows[pl.ds(side * 256 + a * 16 + b, 1)] = line
                    if a != b:
                        rows[pl.ds(side * 256 + b * 16 + a, 1)] = line

    total = jnp.sum(rows[...].T, axis=0, keepdims=True)
    out[...] = total * jnp.float32(1.0 / TOTAL)


def band_kernel(
    field, labels, edge, low, high,
    across_first, across_last, core, lines_across, lines_core, out,
    marks, centre, around, window, once, partner, lines, far_lines, sems,
):
    role = roles()
    odd, is_across, below = role["odd"], role["is_across"], role["below"]
    offset, side = role["offset"], role["side"]
    step = pl.program_id(0)
    at_partner = jnp.where(below == 1, 2, 2 + PLANES)
    at_own = jnp.where(below == 1, 2 + PLANES, 2)
    at_extra = jnp.where(below == 1, 2 + 2 * PLANES, 0)
    at_boundary = at_partner + (1 - odd) * (PLANES - 1)
    boundary = (1 - odd) * (PLANES - 1)
    following = 1 + (1 - odd) * (PLANES - 3)

    far = role["far"]
    from_across, from_core = is_across == 1, is_across == 0

    def fetch(part):
        block = pl.ds(part * PAIR, PAIR)
        source = across_first if part < EARLY // PAIR else across_last
        here = source.at[pl.ds(part * PAIR - (0 if part < EARLY // PAIR else EARLY), PAIR)]
        there = partner.at[block, pl.ds(odd, PLANES - 1)]
        return (
            pltpu.make_async_copy(here, there, sems.at[part]),
            pltpu.make_async_copy(core.at[block], partner.at[block], sems.at[part]),
        )

    near = (
        pltpu.make_async_copy(lines_across, lines, sems.at[K // PAIR]),
        pltpu.make_async_copy(lines_core, lines, sems.at[K // PAIR]),
    )
    extra = pltpu.make_async_copy(lines_across, far_lines, sems.at[K // PAIR + 1])

    def by_role(copies, act):
        for wanted, copy in zip((from_across, from_core), copies):

            @pl.when(wanted)
            def _():
                act(copy)

    @pl.when(step == 0)
    def _():
        by_role(near, lambda copy: copy.start())

        @pl.when(far)
        def _():
            extra.start()

        for part in range(K // PAIR):
            by_role(fetch(part), lambda copy: copy.start())
        by_role(near, lambda copy: copy.wait())

        @pl.when(far)
        def _():
            extra.wait()

    def plane_marks(source, p):
        return source[pl.ds(pl.multiple_of(AT_MARKS + p * ROWS, 8), ROWS)]

    def put_lines(where, index, before, after, p):
        where[index, ROWS : ROWS + 2] = after[2 * p : 2 * p + 2]
        where[index, TALL - 2 :] = before[2 * p : 2 * p + 2]

    def strips(lines, k):
        first = pl.multiple_of(k * STRIP, 8)
        return lines[pl.ds(first, STRIP)], lines[pl.ds(first + LINES, STRIP)]

    def fill_lines(where, k):
        own = pl.ds(pl.multiple_of(k * STRIP, 8), STRIP)
        before, after = low[own], high[own]
        for p in range(PLANES):
            put_lines(where, at_own + p, before, after, p)
        before, after = strips(lines, k)
        for p in range(PLANES):
            put_lines(where, at_partner + p, before, after, p)

        @pl.when(far)
        def _():
            for index, p in ((at_extra + 1 - odd, boundary), (at_extra + odd, following)):
                first = k * STRIP + 2 * p
                where[index, TALL - 2 :] = far_lines[pl.ds(first, 2)]
                where[index, ROWS : ROWS + 2] = far_lines[pl.ds(first + LINES, 2)]

    @pl.when(step == 0)
    def _():
        marks[...] = jnp.full_like(marks, -1.0)
        window[...] = jnp.zeros_like(window)
        fill_lines(marks, K)
        for p in range(PLANES):
            marks[at_own + p, :ROWS] = labels[p].astype(jnp.float32)
            marks[at_partner + p, :ROWS] = plane_marks(lines, p)

        @pl.when(far)
        def _():
            marks[at_extra + 1 - odd, :ROWS] = plane_marks(far_lines, boundary)
            marks[at_extra + odd, :ROWS] = plane_marks(far_lines, following)

        wanted = side.astype(jnp.float32)
        for j in range(PADDED):
            marks[j] = jnp.where(marks[j] == wanted, jnp.float32(1.0), jnp.float32(0.0))
        for j in range(1, WINDOW - 1):
            here = marks[offset + j]
            degree = marks[offset + j - 1] + marks[offset + j + 1] + line_sum(here)
            scaled = here * jnp.float32(SIXTH)
            around[j] = scaled
            centre[j] = scaled * degree

    for part in range(K // PAIR):

        @pl.when(step == part)
        def _():
            by_role(fetch(part), lambda copy: copy.wait())

    def one(i, carry):
        k = step * PAIR + i
        fill_lines(window, k)
        for p in range(PLANES):
            window[at_own + p, :ROWS] = field[i, p]
            window[at_partner + p, :ROWS] = partner[k, p]

        @pl.when(from_across)
        def _():
            window[at_boundary, :ROWS] = edge[k]

        @pl.when(far)
        def _():
            window[at_extra + 1 - odd, :ROWS] = edge[k]
            window[at_extra + odd, :ROWS] = far_lines[
                pl.ds(pl.multiple_of(AT_EXTRA + k * ROWS, 8), ROWS)
            ]

        before = window[offset] * marks[offset]
        here = window[offset + 1] * marks[offset + 1]
        for j in range(1, WINDOW - 1):
            after = window[offset + j + 1] * marks[offset + j + 1]
            once[j] = centre[j] * here - around[j] * (before + after + line_sum(here))
            before, here = here, after
        for j in range(2, WINDOW - 2):
            here = once[j]
            total = once[j - 1] + once[j + 1] + line_sum(here)
            out[i, j - 2] = (centre[j] * here - around[j] * total)[:ROWS]
        return carry

    lax.fori_loop(0, PAIR, one, 0)


def band(field, across_first, across_last, core, labels, edge, low, high,
         lines_across, lines_core):
    return pl.pallas_call(
        band_kernel,
        grid=(K // PAIR,),
        in_specs=[pl.BlockSpec((PAIR, PLANES, ROWS, COLS), lambda i: (i, 0, 0, 0))]
        + [full_spec()] * 4
        + [pl.BlockSpec(memory_space=pl.ANY)] * 5,
        out_specs=pl.BlockSpec((PAIR, BAND, ROWS, COLS), lambda i: (i, 0, 0, 0)),
        out_shape=jax.ShapeDtypeStruct((K, BAND, ROWS, COLS), jnp.float32),
        scratch_shapes=[
            pltpu.VMEM((PADDED, TALL, COLS), jnp.float32),
            pltpu.VMEM((WINDOW, TALL, COLS), jnp.float32),
            pltpu.VMEM((WINDOW, TALL, COLS), jnp.float32),
            pltpu.VMEM((PADDED, TALL, COLS), jnp.float32),
            pltpu.VMEM((WINDOW, TALL, COLS), jnp.float32),
            pltpu.VMEM((K, PLANES, ROWS, COLS), jnp.float32),
            pltpu.VMEM((MESSAGE, COLS), jnp.float32),
            pltpu.VMEM((MESSAGE, COLS), jnp.float32),
            pltpu.SemaphoreType.DMA((K // PAIR + 2,)),
        ],
        compiler_params=pltpu.CompilerParams(vmem_limit_bytes=VMEM_LIMIT),
        cost_estimate=CHEAP,
        name="band",
    )(field, labels, edge, low, high, across_first, across_last, core,
      lines_across, lines_core)


def pack(field, labels):
    lines = jax.ShapeDtypeStruct((LINES, COLS), jnp.float32)
    hbm = pl.BlockSpec(memory_space=pl.ANY)
    return pl.pallas_call(
        pack_kernel,
        in_specs=[full_spec(), full_spec()],
        out_specs=[hbm, hbm, full_spec(), full_spec()],
        out_shape=[
            jax.ShapeDtypeStruct((EDGE, ROWS, COLS), jnp.float32),
            jax.ShapeDtypeStruct((EDGE, ROWS, COLS), jnp.float32),
            lines, lines,
        ],
        scratch_shapes=[
            pltpu.VMEM((PLANES, ROWS, COLS), jnp.float32),
            pltpu.SemaphoreType.DMA((4,)),
        ],
        compiler_params=pltpu.CompilerParams(vmem_limit_bytes=VMEM_LIMIT),
        cost_estimate=CHEAP,
        name="pack",
    )(field, labels)


def trim_kernel(field, labels, first, last, message, flat, sems):
    odd = roles()["odd"]
    planes = pl.ds(1 - odd, PLANES - 1)
    following = 1 + odd * (PLANES - 3)
    copies = [
        pltpu.make_async_copy(field.at[pl.ds(0, EARLY), planes], first, sems.at[0]),
        pltpu.make_async_copy(field.at[pl.ds(EARLY, K - EARLY), planes], last, sems.at[1]),
    ]
    for k in range(K):
        copies.append(
            pltpu.make_async_copy(
                field.at[k, following],
                message.at[pl.ds(AT_EXTRA + k * ROWS, ROWS)],
                sems.at[3 + k],
            )
        )
    for copy in copies:
        copy.start()
    for p in range(PLANES):
        flat[p * ROWS : (p + 1) * ROWS] = labels[p].astype(jnp.float32)
    marks = pltpu.make_async_copy(
        flat, message.at[pl.ds(AT_MARKS, PLANES * ROWS)], sems.at[2]
    )
    marks.start()
    for copy in copies:
        copy.wait()
    marks.wait()


def trim(field, labels):
    hbm = pl.BlockSpec(memory_space=pl.ANY)
    return pl.pallas_call(
        trim_kernel,
        in_specs=[full_spec(), full_spec()],
        out_specs=[hbm, hbm, hbm],
        out_shape=[
            jax.ShapeDtypeStruct((EARLY, PLANES - 1, ROWS, COLS), jnp.float32),
            jax.ShapeDtypeStruct((K - EARLY, PLANES - 1, ROWS, COLS), jnp.float32),
            jax.ShapeDtypeStruct((MESSAGE, COLS), jnp.float32),
        ],
        scratch_shapes=[
            pltpu.VMEM((PLANES * ROWS, COLS), jnp.float32),
            pltpu.SemaphoreType.DMA((3 + K,)),
        ],
        compiler_params=pltpu.CompilerParams(vmem_limit_bytes=VMEM_LIMIT),
        cost_estimate=CHEAP,
        name="trim",
    )(field, labels)


def gram_terms(field, labels, edge, core_edge, low, high, message):
    hbm = pl.BlockSpec(memory_space=pl.ANY)
    return pl.pallas_call(
        gram_kernel,
        grid=(K // FOLD,),
        in_specs=[
            pl.BlockSpec((FOLD * PLANES * ROWS, COLS), lambda i: (i, 0)),
            full_spec(),
        ] + [full_spec()] * 4 + [hbm],
        out_specs=[full_spec(), hbm],
        input_output_aliases={6: 1},
        out_shape=[
            jax.ShapeDtypeStruct((1, 512), jnp.float32),
            jax.ShapeDtypeStruct((MESSAGE, COLS), jnp.float32),
        ],
        scratch_shapes=[
            pltpu.VMEM((PLANES, TALL, COLS), jnp.float32),
            pltpu.VMEM((7, PLANES, ROWS, COLS), jnp.float32),
            pltpu.VMEM((PLANES, 8, COLS), jnp.float32),
            pltpu.VMEM((K, PLANES, ROWS, COLS), jnp.float32),
            pltpu.VMEM((512, COLS), jnp.float32),
            pltpu.SemaphoreType.DMA((2,)),
        ],
        compiler_params=pltpu.CompilerParams(vmem_limit_bytes=VMEM_LIMIT),
        cost_estimate=CHEAP,
        name="gram",
    )(field.reshape(FIELD_ROWS, COLS), labels, edge, core_edge, low, high, message)


def per_device(field, labels):
    edge, core_edge, up, down = pack(field, labels)
    ring = [(i, (i + 1) % 8) for i in range(8)]
    back = [(t, s) for s, t in ring]
    low = lax.ppermute(up, LANE, ring)
    high = lax.ppermute(down, LANE, back)
    edge = lax.ppermute(edge, CHAIN, ACROSS)
    core_edge = lax.ppermute(core_edge, CHAIN, ON_CHIP)
    later, _ = lax.optimization_barrier((field, core_edge))
    first, last, message = trim(later, labels)
    across_first = lax.ppermute(first, CHAIN, BULK_ACROSS)
    core = lax.ppermute(field, CHAIN, ON_CHIP)

    gram, both_lines = gram_terms(
        field, labels, edge, core_edge, low, high, message
    )
    last, _ = lax.optimization_barrier((last, gram))
    lines_across = lax.ppermute(both_lines, CHAIN, ACROSS)
    across_last = lax.ppermute(last, CHAIN, BULK_ACROSS)
    lines_core = lax.ppermute(both_lines, CHAIN, ON_CHIP)

    def swap(value, axes, size, flip):
        return value + lax.ppermute(value, axes, [(i, i ^ flip) for i in range(size)])

    gram, across_first = lax.optimization_barrier((gram, across_first))
    gram = swap(gram, ("core",), 2, 1)
    gram = swap(gram, ("y_near",), 2, 1)
    gram = swap(gram, ("y_far", "y_near"), 4, 3)
    gram = swap(gram, ("z",), 4, 1)
    gram = swap(gram, ("z",), 4, 3)
    gram, core = lax.optimization_barrier((gram, core))
    gram = swap(gram, ("x",), 4, 1)
    gram = swap(gram, ("x",), 4, 3)

    image = band(field, across_first, across_last, core, labels, edge, low, high,
                 lines_across, lines_core)
    return image, gram.reshape(2, K, K)


def solution(mesh):
    finer = Mesh(
        mesh.devices.reshape(2, 4, 2, 4, 2), ("y_far", "x", "core", "z", "y_near")
    )
    return jax.shard_map(
        per_device,
        mesh=finer,
        in_specs=(P(None, CHAIN, LANE, None), P(CHAIN, LANE, None)),
        out_specs=(P(None, CHAIN, LANE, None), P()),
        check_vma=False,
    )
```

```python
import functools

import jax
import jax.numpy as jnp
from jax import lax
from jax.experimental import pallas as pl
from jax.experimental.pallas import tpu as pltpu
from jax.sharding import Mesh
from jax.sharding import PartitionSpec as P

CHAIN = ("y_far", "x", "core")
LANE = ("z", "y_near")
K = 16
PLANES = 12
BAND = 15
STRIP = 2 * PLANES
ROWS = 32
COLS = 128
WINDOW = BAND + 4
PADDED = 2 * PLANES + 4
TALL = ROWS + 8
FOLD = 4
EARLY = 8
PAIR = 4
EDGE = K + 1
LINES = (K + 1) * STRIP
AT_EXTRA = 2 * LINES
AT_MARKS = AT_EXTRA + K * ROWS
MESSAGE = AT_MARKS + PLANES * ROWS
FIELD_ROWS = K * PLANES * ROWS
CHEAP = pl.CostEstimate(flops=1000, bytes_accessed=1000, transcendentals=0)
SIXTH = 1.0 / 6.0
TOTAL = 3932160.0
VMEM_LIMIT = 24 * 1024 * 1024

ACROSS = [(c, (c - 1) % 16 if c % 2 == 0 else (c + 1) % 16) for c in range(16)]
ON_CHIP = [(c, c ^ 1) for c in range(16)]
NEEDS_ACROSS = (4, 6, 12, 14, 1, 3, 9, 11)
BULK_ACROSS = [(s, t) for s, t in ACROSS if t in NEEDS_ACROSS]


def roles():
    c = lax.axis_index("y_far") * 8 + lax.axis_index("x") * 2 + lax.axis_index("core")
    odd = lax.rem(c, 2)
    below = lax.rem(c // 4, 2)
    return dict(
        odd=odd,
        below=below,
        is_across=jnp.where(below == 1, 1 - odd, odd),
        offset=3 * lax.rem(c, 4),
        far=(lax.rem(c, 8) == 0) | (lax.rem(c, 8) == 7),
        side=jnp.where((c >= 4) & (c < 12), 0, 1),
        has=((c >= 3) & (c <= 12), (c <= 4) | (c >= 11)),
    )


def full_spec():
    return pl.BlockSpec(memory_space=pltpu.VMEM)


def smem_spec():
    return pl.BlockSpec(memory_space=pltpu.SMEM)


def pack_kernel(field, labels, edge, core_edge, up, down, marks, sems):
    odd = roles()["odd"]
    last = PLANES - 1
    copies = [
        pltpu.make_async_copy(field.at[:, odd * last], edge.at[pl.ds(0, K)], sems.at[0]),
        pltpu.make_async_copy(
            field.at[:, (1 - odd) * last], core_edge.at[pl.ds(0, K)], sems.at[1]
        ),
    ]
    for copy in copies:
        copy.start()
    late = [
        pltpu.make_async_copy(marks.at[odd * last], edge.at[K], sems.at[2]),
        pltpu.make_async_copy(marks.at[(1 - odd) * last], core_edge.at[K], sems.at[3]),
    ]
    values = [labels[p].astype(jnp.float32) for p in range(PLANES)]
    for p in range(PLANES):
        marks[p] = values[p]
    for copy in late:
        copy.start()
    up[K * STRIP :] = jnp.concatenate([v[ROWS - 2 :] for v in values], axis=0)
    down[K * STRIP :] = jnp.concatenate([v[:2] for v in values], axis=0)

    def one(k, carry):
        strip = pl.ds(pl.multiple_of(k * STRIP, 8), STRIP)
        up[strip] = jnp.concatenate(
            [field[k, p, ROWS - 2 :] for p in range(PLANES)], axis=0
        )
        down[strip] = jnp.concatenate([field[k, p, :2] for p in range(PLANES)], axis=0)
        return carry

    lax.fori_loop(0, K, one, 0)
    for copy in copies + late:
        copy.wait()


def line_sum(here):
    rows = here.shape[0]
    around = pltpu.roll(here, 1, 0) + pltpu.roll(here, rows - 1, 0)
    return around + (pltpu.roll(here, 1, 1) + pltpu.roll(here, COLS - 1, 1))


def gram_kernel(
    field, labels, edge, core_edge, low, high, message, out, lines_out,
    marks, weights, tiles, once, rows, sems,
):
    role = roles()
    odd = role["odd"]
    is_odd = odd == 1
    step = pl.program_id(0)
    steps = K // FOLD
    same = lambda a, b: jnp.where(a == b, jnp.float32(SIXTH), jnp.float32(0.0))
    joins = [
        pltpu.make_async_copy(low, lines_out.at[pl.ds(0, LINES)], sems.at[0]),
        pltpu.make_async_copy(high, lines_out.at[pl.ds(LINES, LINES)], sems.at[1]),
    ]

    @pl.when(step == 0)
    def _():
        for join in joins:
            join.start()
        tiles[...] = jnp.zeros_like(tiles)
        for p in range(PLANES):
            first = K * STRIP + 2 * p
            marks[p, :ROWS] = labels[p].astype(jnp.float32)
            marks[p, ROWS:] = jnp.full((8, COLS), -1.0, jnp.float32)
            marks[p, ROWS : ROWS + 2] = high[first : first + 2]
            marks[p, TALL - 2 :] = low[first : first + 2]
        across_marks = edge[K]
        core_marks = core_edge[K]
        marks_low = jnp.where(is_odd, core_marks, across_marks)
        marks_high = jnp.where(is_odd, across_marks, core_marks)
        for p in range(PLANES):
            tall = marks[p]
            here = tall[:ROWS]
            around = (
                marks[p - 1, :ROWS] if p else marks_low,
                marks[p + 1, :ROWS] if p + 1 < PLANES else marks_high,
                pltpu.roll(tall, 1, 0)[:ROWS],
                pltpu.roll(tall, TALL - 1, 0)[:ROWS],
                pltpu.roll(here, 1, 1),
                pltpu.roll(here, COLS - 1, 1),
            )
            degree = jnp.zeros((ROWS, COLS), jnp.float32)
            for n, other in enumerate(around):
                weight = same(here, other)
                weights[n, p] = weight
                degree = degree + weight
            weights[6, p] = degree

    def one(i, carry):
        k = step * FOLD + i
        across = edge[k]
        core = core_edge[k]
        before = jnp.where(is_odd, core, across)
        last = jnp.where(is_odd, across, core)
        strip = pl.ds(pl.multiple_of(k * STRIP, 8), STRIP)
        after_lines, before_lines = high[strip], low[strip]
        for p in range(PLANES):
            tiles[p, :2] = after_lines[2 * p : 2 * p + 2]
            tiles[p, 6:] = before_lines[2 * p : 2 * p + 2]
        plane = lambda p: field[pl.ds(pl.multiple_of((i * PLANES + p) * ROWS, 8), ROWS)]
        here = plane(0)
        for p in range(PLANES):
            after = plane(p + 1) if p + 1 < PLANES else last
            tall = jnp.concatenate([here, tiles[p]], axis=0)
            value = weights[6, p] * here
            value = value - (weights[0, p] * before + weights[1, p] * after)
            value = value - (
                weights[2, p] * pltpu.roll(tall, 1, 0)[:ROWS]
                + weights[3, p] * pltpu.roll(tall, TALL - 1, 0)[:ROWS]
            )
            once[k, p] = value - (
                weights[4, p] * pltpu.roll(here, 1, 1)
                + weights[5, p] * pltpu.roll(here, COLS - 1, 1)
            )
            before, here = here, after
        return carry

    lax.fori_loop(0, FOLD, one, 0)

    @pl.when(step == steps - 1)
    def _():
        sum_pairs(role, out, marks, once, rows)
        for join in joins:
            join.wait()


def sum_pairs(role, out, marks, once, rows):
    rows[...] = jnp.zeros_like(rows)
    groups = []
    for base in (0, 8):
        groups.append([(base + i, base + j) for i in range(8) for j in range(i, 8)])
    for base in (8, 12):
        groups.append([(i, base + j) for i in range(8) for j in range(4)])
    for side in range(2):

        @pl.when(role["has"][side])
        def _():
            for pairs in groups:
                lefts = sorted({a for a, _ in pairs})
                both = sorted({a for a, _ in pairs} | {b for _, b in pairs})

                def plane(p, sums):
                    sums = list(sums)
                    for t in range(ROWS // 8):
                        window = slice(8 * t, 8 * t + 8)
                        keep = marks[p, window] == jnp.float32(side)
                        values = {k: once[k, p, window] for k in both}
                        kept = {
                            k: jnp.where(keep, values[k], jnp.float32(0.0)) for k in lefts
                        }
                        for n, (a, b) in enumerate(pairs):
                            sums[n] = sums[n] + kept[a] * values[b]
                    return tuple(sums)

                zero = jnp.zeros((8, COLS), jnp.float32)
                sums = lax.fori_loop(0, PLANES, plane, (zero,) * len(pairs))
                for n, (a, b) in enumerate(pairs):
                    line = jnp.sum(sums[n], axis=0, keepdims=True)
                    rows[pl.ds(side * 256 + a * 16 + b, 1)] = line
                    if a != b:
                        rows[pl.ds(side * 256 + b * 16 + a, 1)] = line

    total = jnp.sum(rows[...].T, axis=0, keepdims=True)
    out[...] = total * jnp.float32(1.0 / TOTAL)


def band_kernel(
    labels, edge, low, high,
    field, across_first, across_last, core, lines_across, lines_core, out,
    marks, centre, around, tails, once, stack, lines, far_lines, sems, far_sems,
):
    role = roles()
    odd, is_across, below = role["odd"], role["is_across"], role["below"]
    offset, side = role["offset"], role["side"]
    step = pl.program_id(0)
    at_partner = jnp.where(below == 1, 2, 2 + PLANES)
    at_own = jnp.where(below == 1, 2 + PLANES, 2)
    at_extra = jnp.where(below == 1, 2 + 2 * PLANES, 0)
    at_empty = jnp.where(below == 1, 0, 2 + 2 * PLANES)
    at_boundary = at_partner + (1 - odd) * (PLANES - 1)
    boundary = (1 - odd) * (PLANES - 1)
    following = 1 + (1 - odd) * (PLANES - 3)

    far = role["far"]
    from_across, from_core = is_across == 1, is_across == 0

    parts = K // PAIR

    def fetch(part):
        block = pl.ds(part * PAIR, PAIR)
        early = part < EARLY // PAIR
        source = across_first if early else across_last
        here = source.at[pl.ds(part * PAIR - (0 if early else EARLY), PAIR)]
        there = stack.at[block, pl.ds(at_partner + odd, PLANES - 1)]
        return (
            pltpu.make_async_copy(here, there, sems.at[part]),
            pltpu.make_async_copy(
                core.at[block], stack.at[block, pl.ds(at_partner, PLANES)], sems.at[part]
            ),
        )

    def own(part):
        block = pl.ds(part * PAIR, PAIR)
        return pltpu.make_async_copy(
            field.at[block], stack.at[block, pl.ds(at_own, PLANES)], sems.at[parts + part]
        )

    near = (
        pltpu.make_async_copy(lines_across, lines, sems.at[2 * parts]),
        pltpu.make_async_copy(lines_core, lines, sems.at[2 * parts]),
    )
    extra = pltpu.make_async_copy(lines_across, far_lines, sems.at[2 * parts + 1])
    borders = pltpu.make_async_copy(
        edge.at[pl.ds(0, K)], stack.at[:, at_boundary], sems.at[2 * parts + 2]
    )
    far_planes = [
        pltpu.make_async_copy(
            edge.at[pl.ds(0, K)], stack.at[:, at_extra + 1 - odd], far_sems.at[K]
        )
    ] + [
        pltpu.make_async_copy(
            lines_across.at[pl.ds(AT_EXTRA + k * ROWS, ROWS)],
            stack.at[k, at_extra + odd],
            far_sems.at[k],
        )
        for k in range(K)
    ]

    def by_role(copies, act):
        for wanted, copy in zip((from_across, from_core), copies):

            @pl.when(wanted)
            def _():
                act(copy)

    @pl.when(step == 0)
    def _():
        by_role(near, lambda copy: copy.start())

        @pl.when(far)
        def _():
            extra.start()

        @pl.when(from_across)
        def _():
            borders.start()

        for part in range(parts):
            own(part).start()
            by_role(fetch(part), lambda copy: copy.start())
            if part == 0:

                @pl.when(far)
                def _():
                    for copy in far_planes:
                        copy.start()

        by_role(near, lambda copy: copy.wait())

        @pl.when(far)
        def _():
            extra.wait()

    def plane_marks(source, p):
        return source[pl.ds(pl.multiple_of(AT_MARKS + p * ROWS, 8), ROWS)]

    def strips(source, k):
        first = pl.multiple_of(k * STRIP, 8)
        return source[pl.ds(first, STRIP)], source[pl.ds(first + LINES, STRIP)]

    def fill_lines(where, k, top):
        def put(index, before, after, p):
            where[index, top : top + 2] = after[2 * p : 2 * p + 2]
            where[index, top + 6 : top + 8] = before[2 * p : 2 * p + 2]

        mine = pl.ds(pl.multiple_of(k * STRIP, 8), STRIP)
        before, after = low[mine], high[mine]
        for p in range(PLANES):
            put(at_own + p, before, after, p)
        before, after = strips(lines, k)
        for p in range(PLANES):
            put(at_partner + p, before, after, p)

        @pl.when(far)
        def _():
            for index, p in ((at_extra + 1 - odd, boundary), (at_extra + odd, following)):
                first = k * STRIP + 2 * p
                where[index, top + 6 : top + 8] = far_lines[pl.ds(first, 2)]
                where[index, top : top + 2] = far_lines[pl.ds(first + LINES, 2)]

    @pl.when(step == 0)
    def _():
        marks[...] = jnp.full_like(marks, -1.0)
        tails[...] = jnp.zeros_like(tails)
        for k in range(K):
            for j in range(2):
                stack[k, at_empty + j] = jnp.zeros((ROWS, COLS), jnp.float32)
        fill_lines(marks, K, ROWS)
        for p in range(PLANES):
            marks[at_own + p, :ROWS] = labels[p].astype(jnp.float32)
            marks[at_partner + p, :ROWS] = plane_marks(lines, p)

        @pl.when(far)
        def _():
            marks[at_extra + 1 - odd, :ROWS] = plane_marks(far_lines, boundary)
            marks[at_extra + odd, :ROWS] = plane_marks(far_lines, following)

        wanted = side.astype(jnp.float32)
        for j in range(PADDED):
            marks[j] = jnp.where(marks[j] == wanted, jnp.float32(1.0), jnp.float32(0.0))
        for j in range(1, WINDOW - 1):
            here = marks[offset + j]
            degree = marks[offset + j - 1] + marks[offset + j + 1] + line_sum(here)
            scaled = here * jnp.float32(SIXTH)
            around[j] = scaled
            centre[j] = scaled * degree

    for part in range(parts):

        @pl.when(step == part)
        def _():
            own(part).wait()
            by_role(fetch(part), lambda copy: copy.wait())
            if part == 0:

                @pl.when(from_across)
                def _():
                    borders.wait()

                @pl.when(far)
                def _():
                    for copy in far_planes:
                        copy.wait()

    def one(i, carry):
        k = step * PAIR + i
        fill_lines(tails, k, 0)

        def masked(j):
            whole = jnp.concatenate([stack[k, offset + j], tails[offset + j]], axis=0)
            return whole * marks[offset + j]

        before, here = masked(0), masked(1)
        for j in range(1, WINDOW - 1):
            after = masked(j + 1)
            once[j] = centre[j] * here - around[j] * (before + after + line_sum(here))
            before, here = here, after
        for j in range(2, WINDOW - 2):
            here = once[j]
            total = once[j - 1] + once[j + 1] + line_sum(here)
            out[i, j - 2] = (centre[j] * here - around[j] * total)[:ROWS]
        return carry

    lax.fori_loop(0, PAIR, one, 0)


def band(field, across_first, across_last, core, labels, edge, low, high,
         lines_across, lines_core):
    return pl.pallas_call(
        band_kernel,
        grid=(K // PAIR,),
        in_specs=[full_spec()] * 4 + [pl.BlockSpec(memory_space=pl.ANY)] * 6,
        out_specs=pl.BlockSpec((PAIR, BAND, ROWS, COLS), lambda i: (i, 0, 0, 0)),
        out_shape=jax.ShapeDtypeStruct((K, BAND, ROWS, COLS), jnp.float32),
        scratch_shapes=[
            pltpu.VMEM((PADDED, TALL, COLS), jnp.float32),
            pltpu.VMEM((WINDOW, TALL, COLS), jnp.float32),
            pltpu.VMEM((WINDOW, TALL, COLS), jnp.float32),
            pltpu.VMEM((PADDED, 8, COLS), jnp.float32),
            pltpu.VMEM((WINDOW, TALL, COLS), jnp.float32),
            pltpu.VMEM((K, PADDED, ROWS, COLS), jnp.float32),
            pltpu.VMEM((MESSAGE, COLS), jnp.float32),
            pltpu.VMEM((MESSAGE, COLS), jnp.float32),
            pltpu.SemaphoreType.DMA((2 * (K // PAIR) + 3,)),
            pltpu.SemaphoreType.DMA((K + 1,)),
        ],
        compiler_params=pltpu.CompilerParams(vmem_limit_bytes=VMEM_LIMIT),
        cost_estimate=CHEAP,
        name="band",
    )(labels, edge, low, high, field, across_first, across_last, core,
      lines_across, lines_core)


def pack(field, labels):
    lines = jax.ShapeDtypeStruct((LINES, COLS), jnp.float32)
    hbm = pl.BlockSpec(memory_space=pl.ANY)
    return pl.pallas_call(
        pack_kernel,
        in_specs=[full_spec(), full_spec()],
        out_specs=[hbm, hbm, full_spec(), full_spec()],
        out_shape=[
            jax.ShapeDtypeStruct((EDGE, ROWS, COLS), jnp.float32),
            jax.ShapeDtypeStruct((EDGE, ROWS, COLS), jnp.float32),
            lines, lines,
        ],
        scratch_shapes=[
            pltpu.VMEM((PLANES, ROWS, COLS), jnp.float32),
            pltpu.SemaphoreType.DMA((4,)),
        ],
        compiler_params=pltpu.CompilerParams(vmem_limit_bytes=VMEM_LIMIT),
        cost_estimate=CHEAP,
        name="pack",
    )(field, labels)


def trim_kernel(field, labels, first, last, message, flat, sems):
    odd = roles()["odd"]
    planes = pl.ds(1 - odd, PLANES - 1)
    following = 1 + odd * (PLANES - 3)
    copies = [
        pltpu.make_async_copy(field.at[pl.ds(0, EARLY), planes], first, sems.at[0]),
        pltpu.make_async_copy(field.at[pl.ds(EARLY, K - EARLY), planes], last, sems.at[1]),
    ]
    for k in range(K):
        copies.append(
            pltpu.make_async_copy(
                field.at[k, following],
                message.at[pl.ds(AT_EXTRA + k * ROWS, ROWS)],
                sems.at[3 + k],
            )
        )
    for copy in copies:
        copy.start()
    for p in range(PLANES):
        flat[p * ROWS : (p + 1) * ROWS] = labels[p].astype(jnp.float32)
    marks = pltpu.make_async_copy(
        flat, message.at[pl.ds(AT_MARKS, PLANES * ROWS)], sems.at[2]
    )
    marks.start()
    for copy in copies:
        copy.wait()
    marks.wait()


def trim(field, labels):
    hbm = pl.BlockSpec(memory_space=pl.ANY)
    return pl.pallas_call(
        trim_kernel,
        in_specs=[full_spec(), full_spec()],
        out_specs=[hbm, hbm, hbm],
        out_shape=[
            jax.ShapeDtypeStruct((EARLY, PLANES - 1, ROWS, COLS), jnp.float32),
            jax.ShapeDtypeStruct((K - EARLY, PLANES - 1, ROWS, COLS), jnp.float32),
            jax.ShapeDtypeStruct((MESSAGE, COLS), jnp.float32),
        ],
        scratch_shapes=[
            pltpu.VMEM((PLANES * ROWS, COLS), jnp.float32),
            pltpu.SemaphoreType.DMA((3 + K,)),
        ],
        compiler_params=pltpu.CompilerParams(vmem_limit_bytes=VMEM_LIMIT),
        cost_estimate=CHEAP,
        name="trim",
    )(field, labels)


def gram_terms(field, labels, edge, core_edge, low, high, message):
    hbm = pl.BlockSpec(memory_space=pl.ANY)
    return pl.pallas_call(
        gram_kernel,
        grid=(K // FOLD,),
        in_specs=[
            pl.BlockSpec((FOLD * PLANES * ROWS, COLS), lambda i: (i, 0)),
            full_spec(),
        ] + [full_spec()] * 4 + [hbm],
        out_specs=[full_spec(), hbm],
        input_output_aliases={6: 1},
        out_shape=[
            jax.ShapeDtypeStruct((1, 512), jnp.float32),
            jax.ShapeDtypeStruct((MESSAGE, COLS), jnp.float32),
        ],
        scratch_shapes=[
            pltpu.VMEM((PLANES, TALL, COLS), jnp.float32),
            pltpu.VMEM((7, PLANES, ROWS, COLS), jnp.float32),
            pltpu.VMEM((PLANES, 8, COLS), jnp.float32),
            pltpu.VMEM((K, PLANES, ROWS, COLS), jnp.float32),
            pltpu.VMEM((512, COLS), jnp.float32),
            pltpu.SemaphoreType.DMA((2,)),
        ],
        compiler_params=pltpu.CompilerParams(vmem_limit_bytes=VMEM_LIMIT),
        cost_estimate=CHEAP,
        name="gram",
    )(field.reshape(FIELD_ROWS, COLS), labels, edge, core_edge, low, high, message)


def per_device(field, labels):
    edge, core_edge, up, down = pack(field, labels)
    ring = [(i, (i + 1) % 8) for i in range(8)]
    back = [(t, s) for s, t in ring]
    low = lax.ppermute(up, LANE, ring)
    high = lax.ppermute(down, LANE, back)
    edge = lax.ppermute(edge, CHAIN, ACROSS)
    core_edge = lax.ppermute(core_edge, CHAIN, ON_CHIP)
    later, _ = lax.optimization_barrier((field, core_edge))
    first, last, message = trim(later, labels)
    across_first = lax.ppermute(first, CHAIN, BULK_ACROSS)
    core = lax.ppermute(field, CHAIN, ON_CHIP)

    gram, both_lines = gram_terms(
        field, labels, edge, core_edge, low, high, message
    )
    last, _ = lax.optimization_barrier((last, gram))
    lines_across = lax.ppermute(both_lines, CHAIN, ACROSS)
    across_last = lax.ppermute(last, CHAIN, BULK_ACROSS)
    lines_core = lax.ppermute(both_lines, CHAIN, ON_CHIP)

    def swap(value, axes, size, flip):
        return value + lax.ppermute(value, axes, [(i, i ^ flip) for i in range(size)])

    gram, across_first = lax.optimization_barrier((gram, across_first))
    gram = swap(gram, ("core",), 2, 1)
    gram = swap(gram, ("y_near",), 2, 1)
    gram = swap(gram, ("y_far", "y_near"), 4, 3)
    gram = swap(gram, ("z",), 4, 1)
    gram = swap(gram, ("z",), 4, 3)
    gram, core = lax.optimization_barrier((gram, core))
    gram = swap(gram, ("x",), 4, 1)
    gram = swap(gram, ("x",), 4, 3)

    image = band(field, across_first, across_last, core, labels, edge, low, high,
                 lines_across, lines_core)
    return image, gram.reshape(2, K, K)


def solution(mesh):
    finer = Mesh(
        mesh.devices.reshape(2, 4, 2, 4, 2), ("y_far", "x", "core", "z", "y_near")
    )
    return jax.shard_map(
        per_device,
        mesh=finer,
        in_specs=(P(None, CHAIN, LANE, None), P(CHAIN, LANE, None)),
        out_specs=(P(None, CHAIN, LANE, None), P()),
        check_vma=False,
    )
```

```python
import functools

import jax
import jax.numpy as jnp
from jax import lax
from jax.experimental import pallas as pl
from jax.experimental.pallas import tpu as pltpu
from jax.sharding import Mesh
from jax.sharding import PartitionSpec as P

CHAIN = ("y_far", "x", "core")
LANE = ("z", "y_near")
K = 16
PLANES = 12
BAND = 15
STRIP = 2 * PLANES
ROWS = 32
COLS = 128
WINDOW = BAND + 4
PADDED = 2 * PLANES + 4
TALL = ROWS + 8
FOLD = 16
EARLY = 8
PAIR = 4
EDGE = K + 1
LINES = (K + 1) * STRIP
AT_EXTRA = 2 * LINES
AT_MARKS = AT_EXTRA + K * ROWS
MESSAGE = AT_MARKS + PLANES * ROWS
FIELD_ROWS = K * PLANES * ROWS
CHEAP = pl.CostEstimate(flops=1000, bytes_accessed=1000, transcendentals=0)
SIXTH = 1.0 / 6.0
TOTAL = 3932160.0
VMEM_LIMIT = 24 * 1024 * 1024

ACROSS = [(c, (c - 1) % 16 if c % 2 == 0 else (c + 1) % 16) for c in range(16)]
ON_CHIP = [(c, c ^ 1) for c in range(16)]
NEEDS_ACROSS = (4, 6, 12, 14, 1, 3, 9, 11)
BULK_ACROSS = [(s, t) for s, t in ACROSS if t in NEEDS_ACROSS]


def roles():
    c = lax.axis_index("y_far") * 8 + lax.axis_index("x") * 2 + lax.axis_index("core")
    odd = lax.rem(c, 2)
    below = lax.rem(c // 4, 2)
    return dict(
        odd=odd,
        below=below,
        is_across=jnp.where(below == 1, 1 - odd, odd),
        offset=3 * lax.rem(c, 4),
        far=(lax.rem(c, 8) == 0) | (lax.rem(c, 8) == 7),
        side=jnp.where((c >= 4) & (c < 12), 0, 1),
        has=((c >= 3) & (c <= 12), (c <= 4) | (c >= 11)),
    )


def full_spec():
    return pl.BlockSpec(memory_space=pltpu.VMEM)


def smem_spec():
    return pl.BlockSpec(memory_space=pltpu.SMEM)


def pack_kernel(field, labels, edge, core_edge, up, down, marks, sems):
    odd = roles()["odd"]
    last = PLANES - 1
    copies = [
        pltpu.make_async_copy(field.at[:, odd * last], edge.at[pl.ds(0, K)], sems.at[0]),
        pltpu.make_async_copy(
            field.at[:, (1 - odd) * last], core_edge.at[pl.ds(0, K)], sems.at[1]
        ),
    ]
    for copy in copies:
        copy.start()
    late = [
        pltpu.make_async_copy(marks.at[odd * last], edge.at[K], sems.at[2]),
        pltpu.make_async_copy(marks.at[(1 - odd) * last], core_edge.at[K], sems.at[3]),
    ]
    values = [labels[p].astype(jnp.float32) for p in range(PLANES)]
    for p in range(PLANES):
        marks[p] = values[p]
    for copy in late:
        copy.start()
    up[K * STRIP :] = jnp.concatenate([v[ROWS - 2 :] for v in values], axis=0)
    down[K * STRIP :] = jnp.concatenate([v[:2] for v in values], axis=0)

    def one(k, carry):
        strip = pl.ds(pl.multiple_of(k * STRIP, 8), STRIP)
        up[strip] = jnp.concatenate(
            [field[k, p, ROWS - 2 :] for p in range(PLANES)], axis=0
        )
        down[strip] = jnp.concatenate([field[k, p, :2] for p in range(PLANES)], axis=0)
        return carry

    lax.fori_loop(0, K, one, 0)
    for copy in copies + late:
        copy.wait()


def line_sum(here):
    rows = here.shape[0]
    around = pltpu.roll(here, 1, 0) + pltpu.roll(here, rows - 1, 0)
    return around + (pltpu.roll(here, 1, 1) + pltpu.roll(here, COLS - 1, 1))


def gram_kernel(
    field, labels, edge, core_edge, low, high, message, out, lines_out,
    marks, weights, tiles, once, rows, sems,
):
    role = roles()
    odd = role["odd"]
    is_odd = odd == 1
    step = pl.program_id(0)
    steps = K // FOLD
    same = lambda a, b: jnp.where(a == b, jnp.float32(SIXTH), jnp.float32(0.0))
    joins = [
        pltpu.make_async_copy(low, lines_out.at[pl.ds(0, LINES)], sems.at[0]),
        pltpu.make_async_copy(high, lines_out.at[pl.ds(LINES, LINES)], sems.at[1]),
    ]

    @pl.when(step == 0)
    def _():
        for join in joins:
            join.start()
        tiles[...] = jnp.zeros_like(tiles)
        for p in range(PLANES):
            first = K * STRIP + 2 * p
            marks[p, :ROWS] = labels[p].astype(jnp.float32)
            marks[p, ROWS:] = jnp.full((8, COLS), -1.0, jnp.float32)
            marks[p, ROWS : ROWS + 2] = high[first : first + 2]
            marks[p, TALL - 2 :] = low[first : first + 2]
        across_marks = edge[K]
        core_marks = core_edge[K]
        marks_low = jnp.where(is_odd, core_marks, across_marks)
        marks_high = jnp.where(is_odd, across_marks, core_marks)
        for p in range(PLANES):
            tall = marks[p]
            here = tall[:ROWS]
            around = (
                marks[p - 1, :ROWS] if p else marks_low,
                marks[p + 1, :ROWS] if p + 1 < PLANES else marks_high,
                pltpu.roll(tall, 1, 0)[:ROWS],
                pltpu.roll(tall, TALL - 1, 0)[:ROWS],
                pltpu.roll(here, 1, 1),
                pltpu.roll(here, COLS - 1, 1),
            )
            degree = jnp.zeros((ROWS, COLS), jnp.float32)
            for n, other in enumerate(around):
                weight = same(here, other)
                weights[n, p] = weight
                degree = degree + weight
            weights[6, p] = degree

    def one(i, carry):
        k = step * FOLD + i
        across = edge[k]
        core = core_edge[k]
        before = jnp.where(is_odd, core, across)
        last = jnp.where(is_odd, across, core)
        strip = pl.ds(pl.multiple_of(k * STRIP, 8), STRIP)
        after_lines, before_lines = high[strip], low[strip]
        for p in range(PLANES):
            tiles[p, :2] = after_lines[2 * p : 2 * p + 2]
            tiles[p, 6:] = before_lines[2 * p : 2 * p + 2]
        plane = lambda p: field[pl.ds(pl.multiple_of((i * PLANES + p) * ROWS, 8), ROWS)]
        here = plane(0)
        for p in range(PLANES):
            after = plane(p + 1) if p + 1 < PLANES else last
            tall = jnp.concatenate([here, tiles[p]], axis=0)
            value = weights[6, p] * here
            value = value - (weights[0, p] * before + weights[1, p] * after)
            value = value - (
                weights[2, p] * pltpu.roll(tall, 1, 0)[:ROWS]
                + weights[3, p] * pltpu.roll(tall, TALL - 1, 0)[:ROWS]
            )
            once[k, p] = value - (
                weights[4, p] * pltpu.roll(here, 1, 1)
                + weights[5, p] * pltpu.roll(here, COLS - 1, 1)
            )
            before, here = here, after
        return carry

    lax.fori_loop(0, FOLD, one, 0)

    @pl.when(step == steps - 1)
    def _():
        sum_pairs(role, out, marks, once, rows)
        for join in joins:
            join.wait()


def sum_pairs(role, out, marks, once, rows):
    rows[...] = jnp.zeros_like(rows)
    groups = []
    for base in (0, 8):
        groups.append([(base + i, base + j) for i in range(8) for j in range(i, 8)])
    for base in (8, 12):
        groups.append([(i, base + j) for i in range(8) for j in range(4)])
    for side in range(2):

        @pl.when(role["has"][side])
        def _():
            for pairs in groups:
                lefts = sorted({a for a, _ in pairs})
                both = sorted({a for a, _ in pairs} | {b for _, b in pairs})

                def plane(p, sums):
                    sums = list(sums)
                    for t in range(ROWS // 8):
                        window = slice(8 * t, 8 * t + 8)
                        keep = marks[p, window] == jnp.float32(side)
                        values = {k: once[k, p, window] for k in both}
                        kept = {
                            k: jnp.where(keep, values[k], jnp.float32(0.0)) for k in lefts
                        }
                        for n, (a, b) in enumerate(pairs):
                            sums[n] = sums[n] + kept[a] * values[b]
                    return tuple(sums)

                zero = jnp.zeros((8, COLS), jnp.float32)
                sums = lax.fori_loop(0, PLANES, plane, (zero,) * len(pairs))
                for n, (a, b) in enumerate(pairs):
                    line = jnp.sum(sums[n], axis=0, keepdims=True)
                    rows[pl.ds(side * 256 + a * 16 + b, 1)] = line
                    if a != b:
                        rows[pl.ds(side * 256 + b * 16 + a, 1)] = line

    total = jnp.sum(rows[...].T, axis=0, keepdims=True)
    out[...] = total * jnp.float32(1.0 / TOTAL)


def band_kernel(
    field, labels, edge, low, high,
    across_first, across_last, core, lines_across, lines_core, out,
    marks, centre, around, window, once,
):
    role = roles()
    odd, is_across, below = role["odd"], role["is_across"], role["below"]
    offset, side = role["offset"], role["side"]
    step = pl.program_id(0)
    at_partner = jnp.where(below == 1, 2, 2 + PLANES)
    at_own = jnp.where(below == 1, 2 + PLANES, 2)
    at_extra = jnp.where(below == 1, 2 + 2 * PLANES, 0)
    at_boundary = at_partner + (1 - odd) * (PLANES - 1)
    boundary = (1 - odd) * (PLANES - 1)
    following = 1 + (1 - odd) * (PLANES - 3)

    far = role["far"]
    from_across, from_core = is_across == 1, is_across == 0

    def plane_marks(source, p):
        return source[pl.ds(pl.multiple_of(AT_MARKS + p * ROWS, 8), ROWS)]

    def put_lines(where, index, before, after, p):
        where[index, ROWS : ROWS + 2] = after[2 * p : 2 * p + 2]
        where[index, TALL - 2 :] = before[2 * p : 2 * p + 2]

    def strips(lines, k):
        first = pl.multiple_of(k * STRIP, 8)
        return lines[pl.ds(first, STRIP)], lines[pl.ds(first + LINES, STRIP)]

    def fill_lines(where, k):
        own = pl.ds(pl.multiple_of(k * STRIP, 8), STRIP)
        before, after = low[own], high[own]
        for p in range(PLANES):
            put_lines(where, at_own + p, before, after, p)
        for wanted, source in ((from_across, lines_across), (from_core, lines_core)):

            @pl.when(wanted)
            def _():
                before, after = strips(source, k)
                for p in range(PLANES):
                    put_lines(where, at_partner + p, before, after, p)

        @pl.when(far)
        def _():
            for index, p in ((at_extra + 1 - odd, boundary), (at_extra + odd, following)):
                first = k * STRIP + 2 * p
                where[index, TALL - 2 :] = lines_across[pl.ds(first, 2)]
                where[index, ROWS : ROWS + 2] = lines_across[pl.ds(first + LINES, 2)]

    @pl.when(step == 0)
    def _():
        marks[...] = jnp.full_like(marks, -1.0)
        window[...] = jnp.zeros_like(window)
        fill_lines(marks, K)
        for p in range(PLANES):
            marks[at_own + p, :ROWS] = labels[p].astype(jnp.float32)
            marks[at_partner + p, :ROWS] = jnp.where(
                from_across, plane_marks(lines_across, p), plane_marks(lines_core, p)
            )

        @pl.when(far)
        def _():
            marks[at_extra + 1 - odd, :ROWS] = plane_marks(lines_across, boundary)
            marks[at_extra + odd, :ROWS] = plane_marks(lines_across, following)

        wanted = side.astype(jnp.float32)
        for j in range(PADDED):
            marks[j] = jnp.where(marks[j] == wanted, jnp.float32(1.0), jnp.float32(0.0))
        for j in range(1, WINDOW - 1):
            here = marks[offset + j]
            degree = marks[offset + j - 1] + marks[offset + j + 1] + line_sum(here)
            scaled = here * jnp.float32(SIXTH)
            around[j] = scaled
            centre[j] = scaled * degree

    early = step < EARLY // PAIR

    def one(i, carry):
        k = step * PAIR + i
        fill_lines(window, k)
        for p in range(PLANES):
            window[at_own + p, :ROWS] = field[k, p]

        for wanted, source, first in (
            (from_across & early, across_first, 0),
            (from_across & jnp.logical_not(early), across_last, EARLY),
        ):

            @pl.when(wanted)
            def _():
                for p in range(PLANES - 1):
                    window[at_partner + odd + p, :ROWS] = source[k - first, p]

        @pl.when(from_core)
        def _():
            for p in range(PLANES):
                window[at_partner + p, :ROWS] = core[k, p]

        @pl.when(from_across)
        def _():
            window[at_boundary, :ROWS] = edge[k]

        @pl.when(far)
        def _():
            window[at_extra + 1 - odd, :ROWS] = edge[k]
            window[at_extra + odd, :ROWS] = lines_across[
                pl.ds(pl.multiple_of(AT_EXTRA + k * ROWS, 8), ROWS)
            ]

        before = window[offset] * marks[offset]
        here = window[offset + 1] * marks[offset + 1]
        for j in range(1, WINDOW - 1):
            after = window[offset + j + 1] * marks[offset + j + 1]
            once[j] = centre[j] * here - around[j] * (before + after + line_sum(here))
            before, here = here, after
        for j in range(2, WINDOW - 2):
            here = once[j]
            total = once[j - 1] + once[j + 1] + line_sum(here)
            out[i, j - 2] = (centre[j] * here - around[j] * total)[:ROWS]
        return carry

    lax.fori_loop(0, PAIR, one, 0)


def band(field, across_first, across_last, core, labels, edge, low, high,
         lines_across, lines_core):
    return pl.pallas_call(
        band_kernel,
        grid=(K // PAIR,),
        in_specs=[full_spec()] * 10,
        out_specs=pl.BlockSpec((PAIR, BAND, ROWS, COLS), lambda i: (i, 0, 0, 0)),
        out_shape=jax.ShapeDtypeStruct((K, BAND, ROWS, COLS), jnp.float32),
        scratch_shapes=[
            pltpu.VMEM((PADDED, TALL, COLS), jnp.float32),
            pltpu.VMEM((WINDOW, TALL, COLS), jnp.float32),
            pltpu.VMEM((WINDOW, TALL, COLS), jnp.float32),
            pltpu.VMEM((PADDED, TALL, COLS), jnp.float32),
            pltpu.VMEM((WINDOW, TALL, COLS), jnp.float32),
        ],
        compiler_params=pltpu.CompilerParams(vmem_limit_bytes=VMEM_LIMIT),
        cost_estimate=CHEAP,
        name="band",
    )(field, labels, edge, low, high, across_first, across_last, core,
      lines_across, lines_core)


def pack(field, labels):
    lines = jax.ShapeDtypeStruct((LINES, COLS), jnp.float32)
    hbm = pl.BlockSpec(memory_space=pl.ANY)
    return pl.pallas_call(
        pack_kernel,
        in_specs=[full_spec(), full_spec()],
        out_specs=[hbm, hbm, full_spec(), full_spec()],
        out_shape=[
            jax.ShapeDtypeStruct((EDGE, ROWS, COLS), jnp.float32),
            jax.ShapeDtypeStruct((EDGE, ROWS, COLS), jnp.float32),
            lines, lines,
        ],
        scratch_shapes=[
            pltpu.VMEM((PLANES, ROWS, COLS), jnp.float32),
            pltpu.SemaphoreType.DMA((4,)),
        ],
        compiler_params=pltpu.CompilerParams(vmem_limit_bytes=VMEM_LIMIT),
        cost_estimate=CHEAP,
        name="pack",
    )(field, labels)


def trim_kernel(field, labels, first, last, message, flat, sems):
    odd = roles()["odd"]
    planes = pl.ds(1 - odd, PLANES - 1)
    following = 1 + odd * (PLANES - 3)
    copies = [
        pltpu.make_async_copy(field.at[pl.ds(0, EARLY), planes], first, sems.at[0]),
        pltpu.make_async_copy(field.at[pl.ds(EARLY, K - EARLY), planes], last, sems.at[1]),
    ]
    for k in range(K):
        copies.append(
            pltpu.make_async_copy(
                field.at[k, following],
                message.at[pl.ds(AT_EXTRA + k * ROWS, ROWS)],
                sems.at[3 + k],
            )
        )
    for copy in copies:
        copy.start()
    for p in range(PLANES):
        flat[p * ROWS : (p + 1) * ROWS] = labels[p].astype(jnp.float32)
    marks = pltpu.make_async_copy(
        flat, message.at[pl.ds(AT_MARKS, PLANES * ROWS)], sems.at[2]
    )
    marks.start()
    for copy in copies:
        copy.wait()
    marks.wait()


def trim(field, labels):
    hbm = pl.BlockSpec(memory_space=pl.ANY)
    return pl.pallas_call(
        trim_kernel,
        in_specs=[full_spec(), full_spec()],
        out_specs=[hbm, hbm, hbm],
        out_shape=[
            jax.ShapeDtypeStruct((EARLY, PLANES - 1, ROWS, COLS), jnp.float32),
            jax.ShapeDtypeStruct((K - EARLY, PLANES - 1, ROWS, COLS), jnp.float32),
            jax.ShapeDtypeStruct((MESSAGE, COLS), jnp.float32),
        ],
        scratch_shapes=[
            pltpu.VMEM((PLANES * ROWS, COLS), jnp.float32),
            pltpu.SemaphoreType.DMA((3 + K,)),
        ],
        compiler_params=pltpu.CompilerParams(vmem_limit_bytes=VMEM_LIMIT),
        cost_estimate=CHEAP,
        name="trim",
    )(field, labels)


def gram_terms(field, labels, edge, core_edge, low, high, message):
    hbm = pl.BlockSpec(memory_space=pl.ANY)
    return pl.pallas_call(
        gram_kernel,
        grid=(K // FOLD,),
        in_specs=[
            full_spec(),
            full_spec(),
        ] + [full_spec()] * 4 + [hbm],
        out_specs=[full_spec(), hbm],
        input_output_aliases={6: 1},
        out_shape=[
            jax.ShapeDtypeStruct((1, 512), jnp.float32),
            jax.ShapeDtypeStruct((MESSAGE, COLS), jnp.float32),
        ],
        scratch_shapes=[
            pltpu.VMEM((PLANES, TALL, COLS), jnp.float32),
            pltpu.VMEM((7, PLANES, ROWS, COLS), jnp.float32),
            pltpu.VMEM((PLANES, 8, COLS), jnp.float32),
            pltpu.VMEM((K, PLANES, ROWS, COLS), jnp.float32),
            pltpu.VMEM((512, COLS), jnp.float32),
            pltpu.SemaphoreType.DMA((2,)),
        ],
        compiler_params=pltpu.CompilerParams(vmem_limit_bytes=VMEM_LIMIT),
        cost_estimate=CHEAP,
        name="gram",
    )(field.reshape(FIELD_ROWS, COLS), labels, edge, core_edge, low, high, message)


def per_device(field, labels):
    edge, core_edge, up, down = pack(field, labels)
    ring = [(i, (i + 1) % 8) for i in range(8)]
    back = [(t, s) for s, t in ring]
    low = lax.ppermute(up, LANE, ring)
    high = lax.ppermute(down, LANE, back)
    edge = lax.ppermute(edge, CHAIN, ACROSS)
    core_edge = lax.ppermute(core_edge, CHAIN, ON_CHIP)
    later, _ = lax.optimization_barrier((field, core_edge))
    first, last, message = trim(later, labels)
    across_first = lax.ppermute(first, CHAIN, BULK_ACROSS)
    core = lax.ppermute(field, CHAIN, ON_CHIP)

    gram, both_lines = gram_terms(
        field, labels, edge, core_edge, low, high, message
    )
    last, _ = lax.optimization_barrier((last, gram))
    lines_across = lax.ppermute(both_lines, CHAIN, ACROSS)
    across_last = lax.ppermute(last, CHAIN, BULK_ACROSS)
    lines_core = lax.ppermute(both_lines, CHAIN, ON_CHIP)

    def swap(value, axes, size, flip):
        return value + lax.ppermute(value, axes, [(i, i ^ flip) for i in range(size)])

    gram, across_first = lax.optimization_barrier((gram, across_first))
    gram = swap(gram, ("core",), 2, 1)
    gram = swap(gram, ("y_near",), 2, 1)
    gram = swap(gram, ("y_far", "y_near"), 4, 3)
    gram = swap(gram, ("z",), 4, 1)
    gram = swap(gram, ("z",), 4, 3)
    gram, core = lax.optimization_barrier((gram, core))
    gram = swap(gram, ("x",), 4, 1)
    gram = swap(gram, ("x",), 4, 3)

    image = band(field, across_first, across_last, core, labels, edge, low, high,
                 lines_across, lines_core)
    return image, gram.reshape(2, K, K)


def solution(mesh):
    finer = Mesh(
        mesh.devices.reshape(2, 4, 2, 4, 2), ("y_far", "x", "core", "z", "y_near")
    )
    return jax.shard_map(
        per_device,
        mesh=finer,
        in_specs=(P(None, CHAIN, LANE, None), P(CHAIN, LANE, None)),
        out_specs=(P(None, CHAIN, LANE, None), P()),
        check_vma=False,
    )
```
